256 devices in a mesh: dp: 4 (over y_lo, core), pipe: 8 (over z), tensor: 8 (over x, y_hi).
Axes of the slice: x: 4, y: 4 (y_hi: 2, y_lo: 2; y = y_hi * 2 + y_lo), z: 8, core: 2. Of those that a mesh axis runs over, the one named last changes fastest.
Arguments:
- checkpoint: bfloat16 [8, 4, 192, 7168], P('pipe', 'dp', None, 'tensor'), may hold values from -6 to 6
- projection: bfloat16 [8, 7168, 3, 7168], P('pipe', 'dp', None, 'tensor'), may hold values from -0.0625 to 0.0625
- ctx_grad: bfloat16 [8, 4, 192, 7168], P('pipe', 'dp', None, 'tensor'), may hold values from -6 to 6
- slopes: float32 [56], P('tensor'), may hold values from 0.003 to 0.1
Outputs:
- input_grad: bfloat16 [8, 4, 192, 7168], P('pipe', 'dp', None, 'tensor')
The draws below stay inside these ranges and needn't reach their ends.
All inputs are finite; a program needn't handle non-finite values.
Results may differ from the reference program's by a relative error of at most 0.019.
Values may be sent and summed in bfloat16 or wider, within the bound.
No kernel may reach another device: no remote copies, remote signals or barrier semaphores. Data moves between devices by JAX's collectives and lax.ppermute only.
A program may use at most 128 MiB of HBM per device.

```python
import math
import jax
import jax.numpy as jnp
from jax import lax

D = 7168
HEADS = 56
HD = 128
SEQ = 192
SECTIONS = 8
REPLICAS = 4


def block_scale(rng, extent, pieces, low, largest):
    gain, own = 1.0, jax.random.fold_in(rng, 6)
    for position, parts in pieces:
        steps = jnp.exp(jax.random.uniform(jax.random.fold_in(own, position), (parts,), jnp.float32, low / len(pieces), largest / len(pieces)))
        gain = gain * jnp.repeat(steps, extent[position] // parts).reshape([-1 if axis == position else 1 for axis in range(len(extent))])
    return gain


def normal_values(rng, dims, deviation, bound, pieces=(), dtype=jnp.bfloat16):
    gain = block_scale(rng, dims, pieces, -0.22, 0.18) if pieces else 1.0
    result = jax.random.normal(rng, dims, jnp.float32) * deviation * gain
    return jnp.minimum(jnp.maximum(result, -bound), bound).astype(dtype)


def setup_inputs(seed: int = 0) -> dict:
    streams_of = jax.random.split(jax.random.key(seed), 5)
    return {
        "checkpoint": normal_values(streams_of[0], (SECTIONS, REPLICAS, SEQ, D), 1.0, 6.0, ((0, 8), (1, 4), (3, 8))),
        "projection": normal_values(streams_of[1], (SECTIONS, D, 3, HEADS * HD), D ** -0.5, 0.0625, ((0, 8), (1, 4), (3, 8))),
        "ctx_grad": normal_values(streams_of[2], (SECTIONS, REPLICAS, SEQ, HEADS * HD), 1.0, 6.0, ((0, 8), (1, 4), (3, 8))),
        "slopes": jnp.clip(jnp.exp(math.log(0.1) - 3.506558 * jax.random.uniform(streams_of[3], (HEADS,), jnp.float32) ** block_scale(streams_of[3], (HEADS,), ((0, 8),), -0.2, 0.2)), 0.003, 0.1),
    }


def section_grad(x, w, dctx, slopes):
    f32 = jnp.float32
    bf = jnp.bfloat16
    width = HEADS * HD
    qkv = jnp.dot(x, w.reshape(D, 3 * width), preferred_element_type=f32).astype(bf).reshape(SEQ, 3, HEADS, HD)
    query, keys, values = (qkv[:, 0], qkv[:, 1], qkv[:, 2])
    scale = HD ** (-0.5)
    pos = jnp.arange(SEQ)
    dist = (pos[:, None] - pos[None, :]).astype(f32)
    causal = dist >= 0
    scores = jnp.einsum('qhe,khe->hqk', query.astype(f32), keys.astype(f32)) * scale - slopes[:, None, None] * dist[None]
    scores = jnp.where(causal[None], scores, -1e+30)
    top = lax.optimization_barrier(jnp.max(scores, axis=-1, keepdims=True))
    expo = jnp.where(causal[None], jnp.exp(scores - top), 0.0)
    probs = expo / lax.optimization_barrier(jnp.sum(expo, axis=-1, keepdims=True))
    probs_b = probs.astype(bf)
    grads = dctx.reshape(SEQ, HEADS, HD)
    dprobs = jnp.einsum('qhe,khe->hqk', grads.astype(f32), values.astype(f32))
    delta = lax.optimization_barrier(jnp.sum(probs * dprobs, axis=-1, keepdims=True))
    dscore = (probs * (dprobs - delta) * scale).astype(bf)
    dq = jnp.einsum('hqk,khe->qhe', dscore.astype(f32), keys.astype(f32)).astype(bf)
    dk = jnp.einsum('hqk,qhe->khe', dscore.astype(f32), query.astype(f32)).astype(bf)
    dv = jnp.einsum('hqk,qhe->khe', probs_b.astype(f32), grads.astype(f32)).astype(bf)
    dqkv = jnp.stack([dq, dk, dv], axis=1).reshape(SEQ, 3 * width)
    back = lax.dot_general(dqkv, w.reshape(D, 3 * width), (((1,), (1,)), ((), ())), preferred_element_type=f32)
    return back.astype(bf)

def reference(checkpoint, projection, ctx_grad, slopes):

    def one_section(args):
        xs, w, gs = args
        return lax.map(lambda pair: section_grad(pair[0], w, pair[1], slopes), (xs, gs))
    grads = lax.map(one_section, (checkpoint, projection, ctx_grad))
    return jnp.roll(grads, -1, axis=0)
```

```python
import functools

import jax
import jax.numpy as jnp
from jax import lax
from jax.experimental import pallas as pl
from jax.experimental.pallas import tpu as pltpu
from jax.sharding import PartitionSpec as P

F32 = jnp.float32
BF = jnp.bfloat16
VMEM = pl.BlockSpec(memory_space=pltpu.VMEM)
SMEM = pl.BlockSpec(memory_space=pltpu.SMEM)
NT = (((1,), (1,)), ((), ()))
TN = (((0,), (0,)), ((), ()))
LIMIT = 48 * 1024 * 1024


def is_root(dp, tensor):
    return (tensor >> 2) == (dp >> 1)


def exchange(value, dp_flip, tensor_flip, senders=None):
    pairs = []
    for dp in range(4):
        for tensor in range(8):
            if senders is None or is_root(dp, tensor) == senders:
                pairs.append((dp * 8 + tensor, (dp ^ dp_flip) * 8 + (tensor ^ tensor_flip)))
    return lax.ppermute(value, ("dp", "tensor"), pairs)


def project_body(where_ref, a_ref, b_ref, c_ref, d_ref, mine_ref, theirs_ref, out_ref, rows_ref):
    width = a_ref.shape[1]
    for slot, ref in enumerate((a_ref, b_ref, c_ref, d_ref)):
        side = where_ref[slot // 2]
        half = where_ref[2 + slot % 2]
        rows_ref[side, :, pl.ds(pl.multiple_of(half * width, 128), width)] = ref[...]
    for part in range(3):
        total = jnp.dot(rows_ref[0], mine_ref[part], preferred_element_type=F32)
        total += jnp.dot(rows_ref[1], theirs_ref[part], preferred_element_type=F32)
        out_ref[part] = total.astype(out_ref.dtype)


def project(where, blocks, mine, theirs, dtype):
    length, width = blocks[0].shape
    return pl.pallas_call(
        project_body,
        out_shape=jax.ShapeDtypeStruct((3, length, width), dtype),
        in_specs=[SMEM] + [VMEM] * 6,
        out_specs=VMEM,
        scratch_shapes=[pltpu.VMEM((2, length, 2 * width), BF)],
        compiler_params=pltpu.CompilerParams(vmem_limit_bytes=LIMIT),
        cost_estimate=pl.CostEstimate(
            flops=2 * length * 4 * width * 3 * width, bytes_accessed=24 * width * width, transcendentals=0
        ),
        name="project",
    )(where, *blocks, mine, theirs)


def attend_body(scale, slopes_ref, mine_ref, theirs_ref, ctx_ref, out_ref):
    length = mine_ref.shape[1]
    head = pl.program_id(0)
    query, keys, values = (
        (mine_ref[part] + theirs_ref[part].astype(F32)).astype(BF) for part in range(3)
    )
    grads = ctx_ref[...]
    rows = lax.broadcasted_iota(jnp.int32, (length, length), 0)
    cols = lax.broadcasted_iota(jnp.int32, (length, length), 1)
    dist = (rows - cols).astype(F32)
    causal = rows >= cols
    scores = lax.dot_general(query, keys, NT, preferred_element_type=F32) * scale - slopes_ref[head] * dist
    scores = jnp.where(causal, scores, -1e30)
    top = jnp.max(scores, axis=-1, keepdims=True)
    expo = jnp.where(causal, jnp.exp(scores - top), 0.0)
    probs = expo / jnp.sum(expo, axis=-1, keepdims=True)
    dprobs = lax.dot_general(grads, values, NT, preferred_element_type=F32)
    delta = jnp.sum(probs * dprobs, axis=-1, keepdims=True)
    dscore = (probs * (dprobs - delta) * scale).astype(BF)
    out_ref[0] = jnp.dot(dscore, keys, preferred_element_type=F32).astype(BF)
    out_ref[1] = lax.dot_general(dscore, query, TN, preferred_element_type=F32).astype(BF)
    out_ref[2] = lax.dot_general(probs.astype(BF), grads, TN, preferred_element_type=F32).astype(BF)


def attend(slopes, mine, theirs, ctx_grad):
    parts, length, width = mine.shape
    heads = slopes.shape[0]
    size = width // heads
    three = pl.BlockSpec((3, length, size), lambda head: (0, 0, head))
    return pl.pallas_call(
        functools.partial(attend_body, size ** (-0.5)),
        out_shape=jax.ShapeDtypeStruct((parts, length, width), BF),
        grid=(heads,),
        in_specs=[SMEM, three, three, pl.BlockSpec((length, size), lambda head: (0, head))],
        out_specs=three,
        compiler_params=pltpu.CompilerParams(vmem_limit_bytes=LIMIT),
        cost_estimate=pl.CostEstimate(
            flops=10 * length * length * width,
            bytes_accessed=14 * length * width,
            transcendentals=heads * length * length,
        ),
        name="attend",
    )(slopes, mine, theirs, ctx_grad)


def back_body(where_ref, dqkv_ref, mine_ref, theirs_ref, keep_ref, send_ref, rows_ref):
    width = dqkv_ref.shape[2]
    for side, ref in enumerate((mine_ref, theirs_ref)):
        for half in range(2):
            total = None
            for part in range(3):
                term = lax.dot_general(
                    dqkv_ref[part],
                    ref[part, half * width : (half + 1) * width, :],
                    NT,
                    preferred_element_type=F32,
                )
                total = term if total is None else total + term
            rows_ref[side, half] = total
    for half in range(2):
        keep_ref[half] = rows_ref[where_ref[0], where_ref[2 + half]]
        send_ref[half] = rows_ref[where_ref[1], where_ref[2 + half]].astype(BF)


def back(where, dqkv, mine, theirs):
    parts, length, width = dqkv.shape
    return pl.pallas_call(
        back_body,
        out_shape=(
            jax.ShapeDtypeStruct((2, length, width), F32),
            jax.ShapeDtypeStruct((2, length, width), BF),
        ),
        in_specs=[SMEM] + [VMEM] * 3,
        out_specs=(VMEM, VMEM),
        scratch_shapes=[pltpu.VMEM((2, 2, length, width), F32)],
        compiler_params=pltpu.CompilerParams(vmem_limit_bytes=LIMIT),
        cost_estimate=pl.CostEstimate(
            flops=2 * length * 4 * width * 3 * width, bytes_accessed=24 * width * width, transcendentals=0
        ),
        name="back",
    )(where, dqkv, mine, theirs)


def on_device(checkpoint, projection, ctx_grad, slopes):
    dp = lax.axis_index("dp")
    tensor = lax.axis_index("tensor")
    core = dp & 1
    column_low = (tensor >> 1) & 1
    own_half = tensor & 1
    root = is_root(dp, tensor)
    side = jnp.where(root, column_low, 1 - column_low) ^ core
    where = jnp.stack([side, 1 - side, own_half, 1 - own_half]).astype(jnp.int32)

    mine = jnp.transpose(projection[0], (1, 0, 2))
    own = checkpoint[0, 0]
    near = exchange(own, 2, 0, False)
    far = exchange(own, 2, 1, False)
    same = exchange(own, 0, 1, True)
    theirs = exchange(mine, 1, 0)

    def spread(value):
        first = jnp.where(root, value, exchange(value, 0, 6, True))
        return first, exchange(first, 0, 2)

    near1, near2 = spread(near)
    far1, far2 = spread(far)
    own1, own2 = spread(own)
    same1, same2 = spread(same)
    sent = project(where, (near1, far1, near2, far2), mine, theirs, BF)
    other = exchange(sent, 2, 0)
    kept = project(where, (own1, same1, own2, same2), mine, theirs, F32)
    dqkv = attend(slopes, kept, other, ctx_grad[0, 0])
    dqkv_other = exchange(dqkv, 2, 0)

    def gather_back(dqkv):
        keep, send = back(where, dqkv, mine, theirs)
        total = keep + exchange(send, 0, 2).astype(F32)
        return total + exchange(total.astype(BF), 0, 6, False).astype(F32)

    grads = gather_back(dqkv)
    result_root = grads[0] + exchange(grads[1].astype(BF), 0, 1, True).astype(F32)
    grads = gather_back(dqkv_other).astype(BF)
    result_rest = exchange(grads[0], 2, 0, True).astype(F32) + exchange(grads[1], 2, 1, True).astype(F32)
    result = jnp.where(root, result_root, result_rest).astype(BF)
    pipe = lax.axis_size("pipe")
    result = lax.ppermute(result, "pipe", [(i, (i - 1) % pipe) for i in range(pipe)])
    return result[None, None]


def solution(mesh):
    placed = (
        P("pipe", "dp", None, "tensor"),
        P("pipe", "dp", None, "tensor"),
        P("pipe", "dp", None, "tensor"),
        P("tensor"),
    )
    return jax.shard_map(
        on_device,
        mesh=mesh,
        in_specs=placed,
        out_specs=P("pipe", "dp", None, "tensor"),
        check_vma=False,
    )
```

```python
import functools

import jax
import jax.numpy as jnp
from jax import lax
from jax.experimental import pallas as pl
from jax.experimental.pallas import tpu as pltpu
from jax.sharding import PartitionSpec as P

F32 = jnp.float32
BF = jnp.bfloat16
VMEM = pl.BlockSpec(memory_space=pltpu.VMEM)
SMEM = pl.BlockSpec(memory_space=pltpu.SMEM)
NT = (((1,), (1,)), ((), ()))
TN = (((0,), (0,)), ((), ()))
LIMIT = 20 * 1024 * 1024


def cost(flops, size):
    return pl.CostEstimate(flops=flops // 20, bytes_accessed=size // 20, transcendentals=0)


def is_root(dp, tensor):
    return (tensor >> 2) == (dp >> 1)


def exchange(value, dp_flip, tensor_flip, senders=None):
    pairs = []
    for dp in range(4):
        for tensor in range(8):
            if senders is None or is_root(dp, tensor) == senders:
                pairs.append((dp * 8 + tensor, (dp ^ dp_flip) * 8 + (tensor ^ tensor_flip)))
    return lax.ppermute(value, ("dp", "tensor"), pairs)


def shift(value, tensor_flip=0, senders=None):
    pipe = lax.axis_size("pipe")
    pairs = []
    for stage in range(pipe):
        for dp in range(4):
            for tensor in range(8):
                if senders is None or is_root(dp, tensor) == senders:
                    target = (dp * pipe + (stage - 1) % pipe) * 8 + (tensor ^ tensor_flip)
                    pairs.append(((dp * pipe + stage) * 8 + tensor, target))
    return lax.ppermute(value, ("dp", "pipe", "tensor"), pairs)


def hold_body(after_ref, mine_ref, theirs_ref, *refs):
    del after_ref
    outs, sems = refs[:2], refs[2]
    copies = [
        pltpu.make_async_copy(source, target, sems.at[place])
        for place, (source, target) in enumerate(zip((mine_ref, theirs_ref), outs))
    ]
    for copy in copies:
        copy.start()
    for copy in copies:
        copy.wait()


def hold(after, mine, theirs):
    hbm = pl.BlockSpec(memory_space=pltpu.HBM)
    held = pl.pallas_call(
        hold_body,
        out_shape=(pltpu.VMEM(mine.shape, mine.dtype),) * 2,
        in_specs=[pl.BlockSpec(memory_space=pl.ANY), hbm, hbm],
        out_specs=(VMEM,) * 2,
        scratch_shapes=[pltpu.SemaphoreType.DMA((2,))],
        compiler_params=pltpu.CompilerParams(vmem_limit_bytes=LIMIT),
        cost_estimate=cost(0, 8 * mine.size),
        name="hold",
    )(
        after,
        pltpu.with_memory_space_constraint(mine, pltpu.HBM),
        pltpu.with_memory_space_constraint(theirs, pltpu.HBM),
    )
    return tuple(pltpu.with_memory_space_constraint(value, pltpu.VMEM) for value in held)


def project_body(where_ref, a_ref, b_ref, c_ref, d_ref, mine_ref, theirs_ref, *rest):
    width = a_ref.shape[1]
    out_refs, rows_ref = rest[:-1], rest[-1]
    for slot, ref in enumerate((a_ref, b_ref, c_ref, d_ref)):
        side = where_ref[slot // 2]
        half = where_ref[2 + slot % 2]
        rows_ref[side, :, pl.ds(pl.multiple_of(half * width, 128), width)] = ref[...]
    start = 0
    for out_ref in out_refs:
        stop = start + out_ref.shape[2]
        for part in range(3):
            total = jnp.dot(rows_ref[0], mine_ref[part, :, start:stop], preferred_element_type=F32)
            total += jnp.dot(rows_ref[1], theirs_ref[part, :, start:stop], preferred_element_type=F32)
            out_ref[part] = total.astype(out_ref.dtype)
        start = stop


def project(where, blocks, weights, columns, dtype):
    length, width = blocks[0].shape
    return pl.pallas_call(
        project_body,
        out_shape=tuple(jax.ShapeDtypeStruct((3, length, some), dtype) for some in columns),
        in_specs=[SMEM] + [VMEM] * 6,
        out_specs=(VMEM,) * len(columns),
        scratch_shapes=[pltpu.VMEM((2, length, 2 * width), BF)],
        compiler_params=pltpu.CompilerParams(vmem_limit_bytes=LIMIT),
        cost_estimate=cost(24 * length * width * width, 16 * length * width),
        name="project",
    )(where, *blocks, *weights)


def attend_body(first, scale, slopes_ref, mine_ref, theirs_ref, ctx_ref, out_ref):
    length = mine_ref.shape[1]
    slope = slopes_ref[first + pl.program_id(0)]
    query, keys, values = (
        (mine_ref[part] + theirs_ref[part].astype(F32)).astype(BF) for part in range(3)
    )
    grads = ctx_ref[...]
    rows = lax.broadcasted_iota(jnp.int32, (length, length), 0)
    cols = lax.broadcasted_iota(jnp.int32, (length, length), 1)
    dist = (rows - cols).astype(F32)
    causal = rows >= cols
    scores = lax.dot_general(query, keys, NT, preferred_element_type=F32) * scale - slope * dist
    scores = jnp.where(causal, scores, -1e30)
    top = jnp.max(scores, axis=-1, keepdims=True)
    expo = jnp.where(causal, jnp.exp(scores - top), 0.0)
    probs = expo / jnp.sum(expo, axis=-1, keepdims=True)
    dprobs = lax.dot_general(grads, values, NT, preferred_element_type=F32)
    delta = jnp.sum(probs * dprobs, axis=-1, keepdims=True)
    dscore = (probs * (dprobs - delta) * scale).astype(BF)
    out_ref[0] = jnp.dot(dscore, keys, preferred_element_type=F32).astype(BF)
    out_ref[1] = lax.dot_general(dscore, query, TN, preferred_element_type=F32).astype(BF)
    out_ref[2] = lax.dot_general(probs.astype(BF), grads, TN, preferred_element_type=F32).astype(BF)


def attend(slopes, mine, theirs, ctx_grad, first, size):
    parts, length, width = mine.shape
    three = pl.BlockSpec((3, length, size), lambda head: (0, 0, head))
    return pl.pallas_call(
        functools.partial(attend_body, first, size ** (-0.5)),
        out_shape=jax.ShapeDtypeStruct((parts, length, width), BF),
        grid=(width // size,),
        in_specs=[SMEM, three, three, pl.BlockSpec((length, size), lambda head: (0, first + head))],
        out_specs=three,
        compiler_params=pltpu.CompilerParams(vmem_limit_bytes=LIMIT),
        cost_estimate=cost(10 * length * length * width, 14 * length * width),
        name="attend",
    )(slopes, mine, theirs, ctx_grad)


def back_body(chunks, sets, seeded, where_ref, *refs):
    pieces, refs = refs[: len(chunks)], refs[len(chunks) :]
    weights, refs = refs[:2], refs[2:]
    count = 2 * len(sets)
    seeds, outs = (refs[:count], refs[count:]) if seeded else (None, refs)
    width = outs[0].shape[1]
    for place, slot in enumerate(sets):
        for half in range(2):
            at = pl.ds(pl.multiple_of(where_ref[2 + half] * width, 128), width)
            out_ref = outs[2 * place + half]

            for side, weight in enumerate(weights):

                @pl.when(where_ref[slot] == side)
                def _(weight=weight, at=at, out_ref=out_ref, number=2 * place + half):
                    total = None
                    for (start, stop), piece in zip(chunks, pieces):
                        for part in range(3):
                            term = lax.dot_general(
                                piece[part], weight[part, at, start:stop], NT, preferred_element_type=F32
                            )
                            total = term if total is None else total + term
                    if seeded:
                        total = total + seeds[number][...]
                    out_ref[...] = total.astype(out_ref.dtype)


def back(where, pieces, chunks, weights, sets, dtypes, seeds=()):
    length = pieces[0].shape[1]
    width = weights[0].shape[2]
    depth = sum(stop - start for start, stop in chunks)
    count = 2 * len(sets)
    return pl.pallas_call(
        functools.partial(back_body, chunks, sets, bool(seeds)),
        out_shape=tuple(jax.ShapeDtypeStruct((length, width), dtypes[i // 2]) for i in range(count)),
        in_specs=[SMEM] + [VMEM] * (len(pieces) + 2 + len(seeds)),
        out_specs=(VMEM,) * count,
        compiler_params=pltpu.CompilerParams(vmem_limit_bytes=LIMIT),
        cost_estimate=cost(6 * length * count * width * depth, 6 * length * depth + 4 * count * length * width),
        name="back",
    )(where, *pieces, *weights, *seeds)


def on_device(checkpoint, projection, ctx_grad, slopes):
    dp = lax.axis_index("dp")
    tensor = lax.axis_index("tensor")
    core = dp & 1
    column_low = (tensor >> 1) & 1
    own_half = tensor & 1
    root = is_root(dp, tensor)
    side = jnp.where(root, column_low, 1 - column_low) ^ core
    where = jnp.stack([side, 1 - side, own_half, 1 - own_half]).astype(jnp.int32)

    heads = slopes.shape[0]
    size = ctx_grad.shape[3] // heads
    early = (heads + 1) // 2
    columns = (early * size, (heads - early) * size)
    chunks = ((0, columns[0]), (columns[0], heads * size))

    own = checkpoint[0, 0]
    across = exchange(own, 0, 6)
    mine = jnp.transpose(projection[0], (1, 0, 2))
    theirs = exchange(mine, 1, 0)
    passed1 = jnp.where(root, across, own)
    passed2 = exchange(passed1, 0, 2)
    near1 = exchange(passed1, 2, 0)
    far1 = exchange(passed1, 2, 1)
    near2 = exchange(passed2, 2, 0)
    far2 = exchange(passed2, 2, 1)
    own1 = jnp.where(root, own, across)
    own1, own, _ = lax.optimization_barrier((own1, own, near1))
    own2 = exchange(own1, 0, 2)
    same = exchange(own, 0, 1, True)
    same1 = jnp.where(root, same, exchange(same, 0, 6, True))
    same2 = exchange(same1, 0, 2)

    weights = hold(passed2, mine, theirs)
    sent = project(where, (near1, far1, near2, far2), weights, columns, BF)
    other = [exchange(value, 2, 0) for value in sent]
    kept = project(where, (own1, same1, own2, same2), weights, columns, F32)
    grads = ctx_grad[0, 0]
    dqkv = [attend(slopes, kept[0], other[0], grads, 0, size)]
    grads, _ = lax.optimization_barrier((grads, dqkv[0]))
    dqkv.append(attend(slopes, kept[1], other[1], grads, early, size))
    dqkv_other = [exchange(value, 2, 0) for value in dqkv]

    dqkv, _ = lax.optimization_barrier((dqkv, dqkv_other[0]))
    sets = back(where, dqkv, chunks, weights, (1, 0), (BF, F32))
    swapped = [exchange(value, 0, 2) for value in sets[:2]]
    total = [sets[2 + half] + swapped[half].astype(F32) for half in range(2)]
    total = [value + exchange(value.astype(BF), 0, 6, False).astype(F32) for value in total]
    result_root = total[0] + exchange(total[1].astype(BF), 0, 1, True).astype(F32)

    seeds = back(where, dqkv_other[:1], chunks[:1], weights, (1, 0), (F32, F32))
    second = back(where, dqkv_other[1:], chunks[1:], weights, (1,), (BF,), seeds[:2])
    second = exchange(second[0], 2, 0).astype(F32) + exchange(second[1], 2, 1).astype(F32)
    first = back(where, dqkv_other[1:], chunks[1:], weights, (0,), (BF,), seeds[2:])
    first = exchange(first[0], 2, 0).astype(F32) + exchange(first[1], 2, 1).astype(F32)
    first = first + exchange(second.astype(BF), 0, 2).astype(F32)
    result = jnp.where(root, result_root, first).astype(BF)
    return (shift(result) + shift(first.astype(BF), 6, True))[None, None]


def solution(mesh):
    placed = (
        P("pipe", "dp", None, "tensor"),
        P("pipe", "dp", None, "tensor"),
        P("pipe", "dp", None, "tensor"),
        P("tensor"),
    )
    return jax.shard_map(
        on_device,
        mesh=mesh,
        in_specs=placed,
        out_specs=P("pipe", "dp", None, "tensor"),
        check_vma=False,
    )
```

```python
import functools

import jax
import jax.numpy as jnp
from jax import lax
from jax.experimental import pallas as pl
from jax.experimental.pallas import tpu as pltpu
from jax.sharding import PartitionSpec as P

F32 = jnp.float32
BF = jnp.bfloat16
VMEM = pl.BlockSpec(memory_space=pltpu.VMEM)
SMEM = pl.BlockSpec(memory_space=pltpu.SMEM)
NT = (((1,), (1,)), ((), ()))
TN = (((0,), (0,)), ((), ()))
LIMIT = 20 * 1024 * 1024


def cost(flops, size):
    return pl.CostEstimate(flops=flops // 20, bytes_accessed=size // 20, transcendentals=0)


def is_root(dp, tensor):
    return (tensor >> 2) == (dp >> 1)


def exchange(name, value, dp_flip, tensor_flip, senders=None):
    pairs = []
    for dp in range(4):
        for tensor in range(8):
            if senders is None or is_root(dp, tensor) == senders:
                pairs.append((dp * 8 + tensor, (dp ^ dp_flip) * 8 + (tensor ^ tensor_flip)))
    with jax.named_scope(name):
        return lax.ppermute(value, ("dp", "tensor"), pairs)


def shift(name, value, tensor_flip=0, senders=None):
    pipe = lax.axis_size("pipe")
    pairs = []
    for stage in range(pipe):
        for dp in range(4):
            for tensor in range(8):
                if senders is None or is_root(dp, tensor) == senders:
                    target = (dp * pipe + (stage - 1) % pipe) * 8 + (tensor ^ tensor_flip)
                    pairs.append(((dp * pipe + stage) * 8 + tensor, target))
    with jax.named_scope(name):
        return lax.ppermute(value, ("dp", "pipe", "tensor"), pairs)


def hold_body(after_ref, from_ref, to_ref, sem):
    del after_ref
    copy = pltpu.make_async_copy(from_ref, to_ref, sem)
    copy.start()
    copy.wait()


def hold(after, weight):
    held = pl.pallas_call(
        hold_body,
        out_shape=pltpu.VMEM(weight.shape, weight.dtype),
        in_specs=[pl.BlockSpec(memory_space=pl.ANY), pl.BlockSpec(memory_space=pltpu.HBM)],
        out_specs=VMEM,
        scratch_shapes=[pltpu.SemaphoreType.DMA],
        compiler_params=pltpu.CompilerParams(vmem_limit_bytes=LIMIT),
        cost_estimate=cost(0, 4 * weight.size),
        name="hold",
    )(after, pltpu.with_memory_space_constraint(weight, pltpu.HBM))
    return pltpu.with_memory_space_constraint(held, pltpu.VMEM)


def project_body(columns, slot, seeded, where_ref, near_ref, far_ref, mine_ref, theirs_ref, *refs):
    width = near_ref.shape[1]
    seed_ref, out_ref, rows_ref = (refs[0] if seeded else None), refs[-2], refs[-1]
    for place, ref in enumerate((near_ref, far_ref)):
        half = where_ref[2 + place]
        rows_ref[:, pl.ds(pl.multiple_of(half * width, 128), width)] = ref[...]
    for side, weight in enumerate((mine_ref, theirs_ref)):

        @pl.when(where_ref[slot] == side)
        def _(weight=weight):
            for part in range(3):
                total = jnp.dot(rows_ref[...], weight[part, :, slice(*columns)], preferred_element_type=F32)
                if seeded:
                    total = total + seed_ref[part]
                out_ref[part] = total.astype(out_ref.dtype)


def project(where, blocks, weights, columns, slot, dtype, seed=None):
    length, width = blocks[0].shape
    some = columns[1] - columns[0]
    seeds = () if seed is None else (seed,)
    return pl.pallas_call(
        functools.partial(project_body, columns, slot, bool(seeds)),
        out_shape=jax.ShapeDtypeStruct((3, length, some), dtype),
        in_specs=[SMEM] + [VMEM] * (4 + len(seeds)),
        out_specs=VMEM,
        scratch_shapes=[pltpu.VMEM((length, 2 * width), BF)],
        compiler_params=pltpu.CompilerParams(vmem_limit_bytes=LIMIT),
        cost_estimate=cost(12 * length * width * some, 12 * length * some),
        name="project",
    )(where, *blocks, *weights, *seeds)


def attend_body(first, scale, slopes_ref, mine_ref, theirs_ref, ctx_ref, out_ref):
    length = mine_ref.shape[1]
    slope = slopes_ref[first + pl.program_id(0)]
    query, keys, values = (
        (mine_ref[part] + theirs_ref[part].astype(F32)).astype(BF) for part in range(3)
    )
    grads = ctx_ref[...]
    rows = lax.broadcasted_iota(jnp.int32, (length, length), 0)
    cols = lax.broadcasted_iota(jnp.int32, (length, length), 1)
    dist = (rows - cols).astype(F32)
    causal = rows >= cols
    scores = lax.dot_general(query, keys, NT, preferred_element_type=F32) * scale - slope * dist
    scores = jnp.where(causal, scores, -1e30)
    top = jnp.max(scores, axis=-1, keepdims=True)
    expo = jnp.where(causal, jnp.exp(scores - top), 0.0)
    probs = expo / jnp.sum(expo, axis=-1, keepdims=True)
    dprobs = lax.dot_general(grads, values, NT, preferred_element_type=F32)
    delta = jnp.sum(probs * dprobs, axis=-1, keepdims=True)
    dscore = (probs * (dprobs - delta) * scale).astype(BF)
    out_ref[0] = jnp.dot(dscore, keys, preferred_element_type=F32).astype(BF)
    out_ref[1] = lax.dot_general(dscore, query, TN, preferred_element_type=F32).astype(BF)
    out_ref[2] = lax.dot_general(probs.astype(BF), grads, TN, preferred_element_type=F32).astype(BF)


def attend(slopes, mine, theirs, ctx_grad, first, size):
    parts, length, width = mine.shape
    three = pl.BlockSpec((3, length, size), lambda head: (0, 0, head))
    return pl.pallas_call(
        functools.partial(attend_body, first, size ** (-0.5)),
        out_shape=jax.ShapeDtypeStruct((parts, length, width), BF),
        grid=(width // size,),
        in_specs=[SMEM, three, three, pl.BlockSpec((length, size), lambda head: (0, first + head))],
        out_specs=three,
        compiler_params=pltpu.CompilerParams(vmem_limit_bytes=LIMIT),
        cost_estimate=cost(10 * length * length * width, 14 * length * width),
        name="attend",
    )(slopes, mine, theirs, ctx_grad)


def back_body(chunks, sets, seeded, where_ref, *refs):
    pieces, refs = refs[: len(chunks)], refs[len(chunks) :]
    weights, refs = refs[:2], refs[2:]
    count = 2 * len(sets)
    seeds, outs = (refs[:count], refs[count:]) if seeded else (None, refs)
    width = outs[0].shape[1]
    for place, slot in enumerate(sets):
        for half in range(2):
            at = pl.ds(pl.multiple_of(where_ref[2 + half] * width, 128), width)
            out_ref = outs[2 * place + half]

            for side, weight in enumerate(weights):

                @pl.when(where_ref[slot] == side)
                def _(weight=weight, at=at, out_ref=out_ref, number=2 * place + half):
                    total = None
                    for (start, stop), piece in zip(chunks, pieces):
                        for part in range(3):
                            term = lax.dot_general(
                                piece[part], weight[part, at, start:stop], NT, preferred_element_type=F32
                            )
                            total = term if total is None else total + term
                    if seeded:
                        total = total + seeds[number][...]
                    out_ref[...] = total.astype(out_ref.dtype)


def back(where, pieces, chunks, weights, sets, dtypes, seeds=()):
    length = pieces[0].shape[1]
    width = weights[0].shape[2]
    depth = sum(stop - start for start, stop in chunks)
    count = 2 * len(sets)
    return pl.pallas_call(
        functools.partial(back_body, chunks, sets, bool(seeds)),
        out_shape=tuple(jax.ShapeDtypeStruct((length, width), dtypes[i // 2]) for i in range(count)),
        in_specs=[SMEM] + [VMEM] * (len(pieces) + 2 + len(seeds)),
        out_specs=(VMEM,) * count,
        compiler_params=pltpu.CompilerParams(vmem_limit_bytes=LIMIT),
        cost_estimate=cost(6 * length * count * width * depth, 6 * length * depth + 4 * count * length * width),
        name="back",
    )(where, *pieces, *weights, *seeds)


def on_device(checkpoint, projection, ctx_grad, slopes):
    dp = lax.axis_index("dp")
    tensor = lax.axis_index("tensor")
    core = dp & 1
    column_low = (tensor >> 1) & 1
    own_half = tensor & 1
    root = is_root(dp, tensor)
    side = jnp.where(root, column_low, 1 - column_low) ^ core
    where = jnp.stack([side, 1 - side, own_half, 1 - own_half]).astype(jnp.int32)

    heads = slopes.shape[0]
    size = ctx_grad.shape[3] // heads
    early = heads // 2
    columns = (early * size, (heads - early) * size)
    chunks = ((0, columns[0]), (columns[0], heads * size))

    after = lax.optimization_barrier
    own = checkpoint[0, 0]
    mine = jnp.transpose(projection[0], (1, 0, 2))
    theirs = exchange("theirs", mine, 1, 0)
    across = exchange("across", own, 0, 6)
    same = exchange("same", own, 0, 1, True)
    across, same = after((across, same))
    passed1 = jnp.where(root, across, own)
    own1 = jnp.where(root, own, across)

    near1 = exchange("near1", passed1, 2, 0)
    far1 = exchange("far1", passed1, 2, 1)
    passed2 = exchange("passed2", passed1, 0, 2)
    same1 = exchange("same1", same, 0, 6, True)
    near1, far1, passed2, same1, own1 = after((near1, far1, passed2, same1, own1))
    same1 = jnp.where(root, same, same1)

    near2 = exchange("near2", passed2, 2, 0)
    far2 = exchange("far2", passed2, 2, 1)
    own2 = exchange("own2", own1, 0, 2)
    held_mine = hold(passed1, mine)
    weights = (held_mine, hold(passed2, theirs))
    sums = [project(where, (near1, far1), weights, chunk, 0, F32) for chunk in chunks]
    same1, own2 = after((same1, own2))
    same2 = exchange("same2", same1, 0, 2)

    other = []
    for i in range(2):
        sent = project(where, (near2, far2), weights, chunks[i], 1, BF, sums[i])
        other.append(exchange(f"other{i}", sent, 2, 0))
    kept = [project(where, (own1, same1), weights, chunk, 0, F32) for chunk in chunks]
    kept = [project(where, (own2, same2), weights, chunks[i], 1, F32, kept[i]) for i in range(2)]
    grads = ctx_grad[0, 0]
    dqkv = [attend(slopes, kept[0], other[0], grads, 0, size)]
    other[1], ready = after((other[1], dqkv[0]))
    dqkv_other = [exchange("dqkv0", ready, 2, 0)]
    dqkv.append(attend(slopes, kept[1], other[1], grads, early, size))
    dqkv_other.append(exchange("dqkv1", dqkv[1], 2, 0))

    dqkv, first_arrived = after((dqkv, dqkv_other[0]))
    (sent0, sent1) = back(where, dqkv, chunks, weights, (1,), (BF,))
    swap1 = exchange("own_swap1", sent1, 0, 2)
    total = back(where, dqkv, chunks, weights, (0,), (F32,))
    seeds = back(where, (first_arrived,), chunks[:1], weights, (1, 0), (F32, F32))

    sent0, swap1 = after((sent0, swap1))
    swap0 = exchange("own_swap0", sent0, 0, 2)
    total1 = total[1] + swap1.astype(F32)
    across1 = exchange("own_across1", total1.astype(BF), 0, 6, False)
    dqkv_other[1], _ = after((dqkv_other[1], total))
    swap0, across1 = after((swap0, across1))
    total0 = total[0] + swap0.astype(F32)
    across0 = exchange("own_across0", total0.astype(BF), 0, 6, False)
    total1 = (total1 + across1.astype(F32)).astype(BF)
    far = exchange("own_far", total1, 0, 1, True)
    result_root = total0 + across0.astype(F32) + far.astype(F32)

    second = back(where, dqkv_other[1:], chunks[1:], weights, (1,), (BF,), seeds[:2])
    second = [exchange("second_near", second[0], 2, 0), exchange("second_far", second[1], 2, 1)]
    first = back(where, dqkv_other[1:], chunks[1:], weights, (0,), (BF,), seeds[2:])
    second, first = after((second, first))
    first = [exchange("first_near", first[0], 2, 0), exchange("first_far", first[1], 2, 1)]
    second = second[0].astype(F32) + second[1].astype(F32)
    swapped = exchange("swap", second.astype(BF), 0, 2)
    total = first[0].astype(F32) + first[1].astype(F32) + swapped.astype(F32)
    result = jnp.where(root, result_root, total).astype(BF)
    return (shift("shift", result) + shift("shift_across", total.astype(BF), 6, True))[None, None]


def solution(mesh):
    placed = (
        P("pipe", "dp", None, "tensor"),
        P("pipe", "dp", None, "tensor"),
        P("pipe", "dp", None, "tensor"),
        P("tensor"),
    )
    return jax.shard_map(
        on_device,
        mesh=mesh,
        in_specs=placed,
        out_specs=P("pipe", "dp", None, "tensor"),
        check_vma=False,
    )
```

```python
import functools

import jax
import jax.numpy as jnp
from jax import lax
from jax.experimental import pallas as pl
from jax.experimental.pallas import tpu as pltpu
from jax.sharding import PartitionSpec as P

F32 = jnp.float32
BF = jnp.bfloat16
VMEM = pl.BlockSpec(memory_space=pltpu.VMEM)
SMEM = pl.BlockSpec(memory_space=pltpu.SMEM)
NT = (((1,), (1,)), ((), ()))
TN = (((0,), (0,)), ((), ()))
LIMIT = 20 * 1024 * 1024


def cost(flops, size):
    return pl.CostEstimate(flops=flops // 20, bytes_accessed=size // 20, transcendentals=0)


def is_root(dp, tensor):
    return (tensor >> 2) == (dp >> 1)


def exchange(name, value, dp_flip, tensor_flip, senders=None):
    pairs = []
    for dp in range(4):
        for tensor in range(8):
            if senders is None or is_root(dp, tensor) == senders:
                pairs.append((dp * 8 + tensor, (dp ^ dp_flip) * 8 + (tensor ^ tensor_flip)))
    with jax.named_scope(name):
        return lax.ppermute(value, ("dp", "tensor"), pairs)


def shift(name, value, tensor_flip, senders):
    pipe = lax.axis_size("pipe")
    pairs = []
    for stage in range(pipe):
        for dp in range(4):
            for tensor in range(8):
                if is_root(dp, tensor) == senders:
                    target = (dp * pipe + (stage - 1) % pipe) * 8 + (tensor ^ tensor_flip)
                    pairs.append(((dp * pipe + stage) * 8 + tensor, target))
    with jax.named_scope(name):
        return lax.ppermute(value, ("dp", "pipe", "tensor"), pairs)


def hold_body(after_ref, mine_ref, theirs_ref, *refs):
    del after_ref
    outs, sems = refs[:2], refs[2]
    copies = [
        pltpu.make_async_copy(source, target, sems.at[place])
        for place, (source, target) in enumerate(zip((mine_ref, theirs_ref), outs))
    ]
    for copy in copies:
        copy.start()
    for copy in copies:
        copy.wait()


def hold(after, mine, theirs):
    hbm = pl.BlockSpec(memory_space=pltpu.HBM)
    held = pl.pallas_call(
        hold_body,
        out_shape=(pltpu.VMEM(mine.shape, mine.dtype),) * 2,
        in_specs=[pl.BlockSpec(memory_space=pl.ANY), hbm, hbm],
        out_specs=(VMEM,) * 2,
        scratch_shapes=[pltpu.SemaphoreType.DMA((2,))],
        compiler_params=pltpu.CompilerParams(vmem_limit_bytes=LIMIT),
        cost_estimate=cost(0, 8 * mine.size),
        name="hold",
    )(
        after,
        pltpu.with_memory_space_constraint(mine, pltpu.HBM),
        pltpu.with_memory_space_constraint(theirs, pltpu.HBM),
    )
    return tuple(pltpu.with_memory_space_constraint(value, pltpu.VMEM) for value in held)


def project_body(columns, slot, seeded, where_ref, near_ref, far_ref, mine_ref, theirs_ref, *refs):
    width = near_ref.shape[1]
    seed_ref, out_ref, rows_ref = (refs[0] if seeded else None), refs[-2], refs[-1]
    for place, ref in enumerate((near_ref, far_ref)):
        half = where_ref[2 + place]
        rows_ref[:, pl.ds(pl.multiple_of(half * width, 128), width)] = ref[...]
    for side, weight in enumerate((mine_ref, theirs_ref)):

        @pl.when(where_ref[slot] == side)
        def _(weight=weight):
            for part in range(3):
                total = jnp.dot(rows_ref[...], weight[part, :, slice(*columns)], preferred_element_type=F32)
                if seeded:
                    total = total + seed_ref[part, :, slice(*columns)]
                out_ref[part] = total.astype(out_ref.dtype)


def project(where, blocks, weights, columns, slot, dtype, seed=None):
    length, width = blocks[0].shape
    some = columns[1] - columns[0]
    seeds = () if seed is None else (seed,)
    return pl.pallas_call(
        functools.partial(project_body, columns, slot, bool(seeds)),
        out_shape=jax.ShapeDtypeStruct((3, length, some), dtype),
        in_specs=[SMEM] + [VMEM] * (4 + len(seeds)),
        out_specs=VMEM,
        scratch_shapes=[pltpu.VMEM((length, 2 * width), BF)],
        compiler_params=pltpu.CompilerParams(vmem_limit_bytes=LIMIT),
        cost_estimate=cost(12 * length * width * some, 12 * length * some),
        name="project",
    )(where, *blocks, *weights, *seeds)


def attend_body(first, scale, slopes_ref, mine_ref, upper_ref, lower_ref, ctx_ref, *out_refs):
    length = mine_ref.shape[1]
    slope = slopes_ref[first + pl.program_id(0)]
    query, keys, values = (
        (mine_ref[part] + jnp.concatenate([upper_ref[part], lower_ref[part]]).astype(F32)).astype(BF)
        for part in range(3)
    )
    grads = ctx_ref[...]
    rows = lax.broadcasted_iota(jnp.int32, (length, length), 0)
    cols = lax.broadcasted_iota(jnp.int32, (length, length), 1)
    dist = (rows - cols).astype(F32)
    causal = rows >= cols
    scores = lax.dot_general(query, keys, NT, preferred_element_type=F32) * scale - slope * dist
    scores = jnp.where(causal, scores, -1e30)
    top = jnp.max(scores, axis=-1, keepdims=True)
    expo = jnp.where(causal, jnp.exp(scores - top), 0.0)
    probs = expo / jnp.sum(expo, axis=-1, keepdims=True)
    dprobs = lax.dot_general(grads, values, NT, preferred_element_type=F32)
    delta = jnp.sum(probs * dprobs, axis=-1, keepdims=True)
    dscore = (probs * (dprobs - delta) * scale).astype(BF)
    results = (
        jnp.dot(dscore, keys, preferred_element_type=F32).astype(BF),
        lax.dot_general(dscore, query, TN, preferred_element_type=F32).astype(BF),
        lax.dot_general(probs.astype(BF), grads, TN, preferred_element_type=F32).astype(BF),
    )
    for part, value in enumerate(results):
        out_refs[0][part] = value
        for place, out_ref in enumerate(out_refs[1:]):
            some = out_ref.shape[1]
            out_ref[part] = value[place * some : (place + 1) * some]


def attend(slopes, mine, upper, lower, ctx_grad, first, size, cut):
    parts, length, width = mine.shape

    def block(rows, offset):
        return pl.BlockSpec((3, rows, size), lambda head: (0, 0, head + offset))

    rows = (length, length // 2, length // 2) if cut else (length,)
    return pl.pallas_call(
        functools.partial(attend_body, first, size ** (-0.5)),
        out_shape=tuple(jax.ShapeDtypeStruct((parts, some, width), BF) for some in rows),
        grid=(width // size,),
        in_specs=[
            SMEM,
            block(length, 0),
            block(length // 2, first),
            block(length // 2, 0),
            pl.BlockSpec((length, size), lambda head: (0, first + head)),
        ],
        out_specs=tuple(block(some, 0) for some in rows),
        compiler_params=pltpu.CompilerParams(vmem_limit_bytes=LIMIT),
        cost_estimate=cost(10 * length * length * width, 14 * length * width),
        name="attend",
    )(slopes, mine, upper, lower, ctx_grad)


def back_body(chunks, starts, slot, where_ref, *refs):
    pieces, weights, outs = refs[: len(chunks)], refs[len(chunks) : -2], refs[-2:]
    rows, width = outs[0].shape
    for half, out_ref in enumerate(outs):
        at = pl.ds(pl.multiple_of(where_ref[2 + half] * width, 128), width)
        for side, weight in enumerate(weights):

            @pl.when(where_ref[slot] == side)
            def _(weight=weight, at=at, out_ref=out_ref):
                total = None
                for (start, stop), first, piece in zip(chunks, starts, pieces):
                    for part in range(3):
                        term = lax.dot_general(
                            piece[part, first : first + rows],
                            weight[part, at, start:stop],
                            NT,
                            preferred_element_type=F32,
                        )
                        total = term if total is None else total + term
                out_ref[...] = total.astype(out_ref.dtype)


def back(where, pieces, starts, rows, chunks, weights, slot, dtype):
    width = weights[0].shape[2]
    return pl.pallas_call(
        functools.partial(back_body, chunks, starts, slot),
        out_shape=(jax.ShapeDtypeStruct((rows, width), dtype),) * 2,
        in_specs=[SMEM] + [VMEM] * (len(pieces) + 2),
        out_specs=(VMEM,) * 2,
        compiler_params=pltpu.CompilerParams(vmem_limit_bytes=LIMIT),
        cost_estimate=cost(12 * rows * width * width, 10 * rows * width),
        name="back",
    )(where, *pieces, *weights)


def on_device(checkpoint, projection, ctx_grad, slopes):
    dp = lax.axis_index("dp")
    tensor = lax.axis_index("tensor")
    core = dp & 1
    column_low = (tensor >> 1) & 1
    own_half = tensor & 1
    root = is_root(dp, tensor)
    side = jnp.where(root, column_low, 1 - column_low) ^ core
    where = jnp.stack([side, 1 - side, own_half, 1 - own_half]).astype(jnp.int32)

    heads = slopes.shape[0]
    size = ctx_grad.shape[3] // heads
    early = (heads + 1) // 2
    columns = (early * size, (heads - early) * size)
    chunks = ((0, columns[0]), (columns[0], heads * size))

    after = lax.optimization_barrier
    own = checkpoint[0, 0]
    length = own.shape[0]
    rows = length // 2
    halves = (own[:rows], own[rows:])
    mine = jnp.transpose(projection[0], (1, 0, 2))
    theirs = exchange("theirs", mine, 1, 0)

    across0 = exchange("across0", halves[0], 0, 6)
    same = exchange("same", own, 0, 1, True)
    across0, same, halves1, same_root = after((across0, same, halves[1], same))
    passed0 = jnp.where(root, across0, halves[0])
    near1_0 = exchange("near1_0", passed0, 2, 0)
    far1_0 = exchange("far1_0", passed0, 2, 1)
    passed2_0 = exchange("passed2_0", passed0, 0, 2)
    across1 = exchange("across1", halves1, 0, 6)
    near1_0, far1_0, passed2_0 = after((near1_0, far1_0, passed2_0))

    near2_0 = exchange("near2_0", passed2_0, 2, 0)
    far2_0 = exchange("far2_0", passed2_0, 2, 1)
    passed1 = jnp.where(root, across1, halves1)
    own1 = jnp.where(root, own, jnp.concatenate([across0, across1]))
    passed2_1 = exchange("passed2_1", passed1, 0, 2)
    across1, same_root = after((across1, same_root))
    same1 = jnp.where(root, same_root, exchange("same1", same_root, 0, 6, True))
    weights = hold(passed2_0, mine, theirs)
    everything = (0, chunks[1][1])
    sums = project(where, (near1_0, far1_0), weights, everything, 0, F32)
    near2_0, far2_0, passed1, weights, sums = after((near2_0, far2_0, passed1, weights, sums))

    near1_1 = exchange("near1_1", passed1, 2, 0)
    far1_1 = exchange("far1_1", passed1, 2, 1)
    sent = project(where, (near2_0, far2_0), weights, everything, 1, BF, sums)
    upper = exchange("other_upper", sent, 2, 0)
    passed2_1, own1 = after((passed2_1, own1))
    own2 = exchange("own2", own1, 0, 2)
    near1_1, far1_1, passed2_1, sent = after((near1_1, far1_1, passed2_1, sent))

    near2_1 = exchange("near2_1", passed2_1, 2, 0)
    far2_1 = exchange("far2_1", passed2_1, 2, 1)
    own2, same1 = after((own2, same1))
    same2 = exchange("same2", same1, 0, 2)
    sums = project(where, (near1_1, far1_1), weights, everything, 0, F32)
    lower = []
    for i in range(2):
        sent = project(where, (near2_1, far2_1), weights, chunks[i], 1, BF, sums)
        sent, sums = after((sent, sums))
        lower.append(exchange(f"other_lower{i}", sent, 2, 0))
    kept = project(where, (own1, same1), weights, everything, 0, F32)
    kept = [project(where, (own2, same2), weights, chunk, 1, F32, kept) for chunk in chunks]
    grads = ctx_grad[0, 0]
    (early_dqkv,) = attend(slopes, kept[0], upper, lower[0], grads, 0, size, False)
    lower[1], ready = after((lower[1], early_dqkv))
    early_other = exchange("dqkv0", ready, 2, 0)
    (late_dqkv,) = attend(slopes, kept[1], upper, lower[1], grads, early, size, False)
    late_other = exchange("dqkv1", late_dqkv, 2, 0)

    (early_dqkv, late_dqkv), early_other = after(((early_dqkv, late_dqkv), early_other))
    pieces = (early_dqkv, late_dqkv)
    (sent0, sent1) = back(where, pieces, (0, 0), length, chunks, weights, 1, BF)
    swap1 = exchange("own_swap1", sent1, 0, 2)
    total = back(where, pieces, (0, 0), length, chunks, weights, 0, F32)
    late_other, total = after((late_other, total))
    sent0, swap1 = after((sent0, swap1))
    swap0 = exchange("own_swap0", sent0, 0, 2)
    total1 = total[1] + swap1.astype(F32)
    arrived1 = exchange("own_across1", total1.astype(BF), 0, 6, False)
    swap0, arrived1 = after((swap0, arrived1))
    total0 = total[0] + swap0.astype(F32)
    arrived0 = exchange("own_across0", total0.astype(BF), 0, 6, False)
    total1 = (total1 + arrived1.astype(F32)).astype(BF)
    far = exchange("own_far", total1, 0, 1, True)
    shifted = shift("shift_root", (total0 + arrived0.astype(F32) + far.astype(F32)).astype(BF), 0, True)

    outs = []
    previous = ()
    for i in range(2):
        pieces, starts = (early_other, late_other), (i * rows, i * rows)
        second = back(where, pieces, starts, rows, chunks, weights, 1, BF)
        first = back(where, pieces, starts, rows, chunks, weights, 0, BF)
        second, previous = after((second, previous))
        second = [exchange(f"second_near{i}", second[0], 2, 0), exchange(f"second_far{i}", second[1], 2, 1)]
        second, first = after((second, first))
        first = [exchange(f"first_near{i}", first[0], 2, 0), exchange(f"first_far{i}", first[1], 2, 1)]
        second = second[0].astype(F32) + second[1].astype(F32)
        swapped = exchange(f"swap{i}", second.astype(BF), 0, 2)
        previous = first
        sums = (first[0].astype(F32) + first[1].astype(F32) + swapped.astype(F32)).astype(BF)
        outs.append(
            shift(f"shift{i}", sums, 0, False)
            + shift(f"shift_across{i}", sums, 6, True)
            + shifted[i * rows : (i + 1) * rows]
        )
    return jnp.concatenate(outs)[None, None]


def solution(mesh):
    placed = (
        P("pipe", "dp", None, "tensor"),
        P("pipe", "dp", None, "tensor"),
        P("pipe", "dp", None, "tensor"),
        P("tensor"),
    )
    return jax.shard_map(
        on_device,
        mesh=mesh,
        in_specs=placed,
        out_specs=P("pipe", "dp", None, "tensor"),
        check_vma=False,
    )
```

```python
import functools

import jax
import jax.numpy as jnp
from jax import lax
from jax.experimental import pallas as pl
from jax.experimental.pallas import tpu as pltpu
from jax.sharding import PartitionSpec as P

F32 = jnp.float32
BF = jnp.bfloat16
VMEM = pl.BlockSpec(memory_space=pltpu.VMEM)
SMEM = pl.BlockSpec(memory_space=pltpu.SMEM)
NT = (((1,), (1,)), ((), ()))
TN = (((0,), (0,)), ((), ()))
LIMIT = 20 * 1024 * 1024


def cost(flops, size):
    return pl.CostEstimate(flops=flops // 20, bytes_accessed=size // 20, transcendentals=0)


def is_root(dp, tensor):
    return (tensor >> 2) == (dp >> 1)


def exchange(name, value, dp_flip, tensor_flip, senders=None):
    pairs = []
    for dp in range(4):
        for tensor in range(8):
            if senders is None or is_root(dp, tensor) == senders:
                pairs.append((dp * 8 + tensor, (dp ^ dp_flip) * 8 + (tensor ^ tensor_flip)))
    with jax.named_scope(name):
        return lax.ppermute(value, ("dp", "tensor"), pairs)


def shift(name, value, tensor_flip=0, senders=None):
    pipe = lax.axis_size("pipe")
    pairs = []
    for stage in range(pipe):
        for dp in range(4):
            for tensor in range(8):
                if senders is None or is_root(dp, tensor) == senders:
                    target = (dp * pipe + (stage - 1) % pipe) * 8 + (tensor ^ tensor_flip)
                    pairs.append(((dp * pipe + stage) * 8 + tensor, target))
    with jax.named_scope(name):
        return lax.ppermute(value, ("dp", "pipe", "tensor"), pairs)


def hold_body(after_ref, mine_ref, theirs_ref, *refs):
    del after_ref
    outs, sems = refs[:2], refs[2]
    copies = [
        pltpu.make_async_copy(source, target, sems.at[place])
        for place, (source, target) in enumerate(zip((mine_ref, theirs_ref), outs))
    ]
    for copy in copies:
        copy.start()
    for copy in copies:
        copy.wait()


def hold(after, mine, theirs):
    hbm = pl.BlockSpec(memory_space=pltpu.HBM)
    held = pl.pallas_call(
        hold_body,
        out_shape=(pltpu.VMEM(mine.shape, mine.dtype),) * 2,
        in_specs=[pl.BlockSpec(memory_space=pl.ANY), hbm, hbm],
        out_specs=(VMEM,) * 2,
        scratch_shapes=[pltpu.SemaphoreType.DMA((2,))],
        compiler_params=pltpu.CompilerParams(vmem_limit_bytes=LIMIT),
        cost_estimate=cost(0, 8 * mine.size),
        name="hold",
    )(
        after,
        pltpu.with_memory_space_constraint(mine, pltpu.HBM),
        pltpu.with_memory_space_constraint(theirs, pltpu.HBM),
    )
    return tuple(pltpu.with_memory_space_constraint(value, pltpu.VMEM) for value in held)


def project_body(columns, slot, seeded, where_ref, near_ref, far_ref, mine_ref, theirs_ref, *refs):
    width = near_ref.shape[1]
    seed_ref, out_ref, rows_ref = (refs[0] if seeded else None), refs[-2], refs[-1]
    for place, ref in enumerate((near_ref, far_ref)):
        half = where_ref[2 + place]
        rows_ref[:, pl.ds(pl.multiple_of(half * width, 128), width)] = ref[...]
    for side, weight in enumerate((mine_ref, theirs_ref)):

        @pl.when(where_ref[slot] == side)
        def _(weight=weight):
            for part in range(3):
                total = jnp.dot(rows_ref[...], weight[part, :, slice(*columns)], preferred_element_type=F32)
                if seeded:
                    total = total + seed_ref[part]
                out_ref[part] = total.astype(out_ref.dtype)


def project(where, blocks, weights, columns, slot, dtype, seed=None):
    length, width = blocks[0].shape
    some = columns[1] - columns[0]
    seeds = () if seed is None else (seed,)
    return pl.pallas_call(
        functools.partial(project_body, columns, slot, bool(seeds)),
        out_shape=jax.ShapeDtypeStruct((3, length, some), dtype),
        in_specs=[SMEM] + [VMEM] * (4 + len(seeds)),
        out_specs=VMEM,
        scratch_shapes=[pltpu.VMEM((length, 2 * width), BF)],
        compiler_params=pltpu.CompilerParams(vmem_limit_bytes=LIMIT),
        cost_estimate=cost(12 * length * width * some, 12 * length * some),
        name="project",
    )(where, *blocks, *weights, *seeds)


def attend_body(first, scale, slopes_ref, mine_ref, theirs_ref, ctx_ref, out_ref):
    length = mine_ref.shape[1]
    slope = slopes_ref[first + pl.program_id(0)]
    query, keys, values = (
        (mine_ref[part] + theirs_ref[part].astype(F32)).astype(BF) for part in range(3)
    )
    grads = ctx_ref[...]
    rows = lax.broadcasted_iota(jnp.int32, (length, length), 0)
    cols = lax.broadcasted_iota(jnp.int32, (length, length), 1)
    dist = (rows - cols).astype(F32)
    causal = rows >= cols
    scores = lax.dot_general(query, keys, NT, preferred_element_type=F32) * scale - slope * dist
    scores = jnp.where(causal, scores, -1e30)
    top = jnp.max(scores, axis=-1, keepdims=True)
    expo = jnp.where(causal, jnp.exp(scores - top), 0.0)
    probs = expo / jnp.sum(expo, axis=-1, keepdims=True)
    dprobs = lax.dot_general(grads, values, NT, preferred_element_type=F32)
    delta = jnp.sum(probs * dprobs, axis=-1, keepdims=True)
    dscore = (probs * (dprobs - delta) * scale).astype(BF)
    out_ref[0] = jnp.dot(dscore, keys, preferred_element_type=F32).astype(BF)
    out_ref[1] = lax.dot_general(dscore, query, TN, preferred_element_type=F32).astype(BF)
    out_ref[2] = lax.dot_general(probs.astype(BF), grads, TN, preferred_element_type=F32).astype(BF)


def attend(slopes, mine, theirs, ctx_grad, first, size):
    parts, length, width = mine.shape
    three = pl.BlockSpec((3, length, size), lambda head: (0, 0, head))
    return pl.pallas_call(
        functools.partial(attend_body, first, size ** (-0.5)),
        out_shape=jax.ShapeDtypeStruct((parts, length, width), BF),
        grid=(width // size,),
        in_specs=[SMEM, three, three, pl.BlockSpec((length, size), lambda head: (0, first + head))],
        out_specs=three,
        compiler_params=pltpu.CompilerParams(vmem_limit_bytes=LIMIT),
        cost_estimate=cost(10 * length * length * width, 14 * length * width),
        name="attend",
    )(slopes, mine, theirs, ctx_grad)


def back_body(chunks, sets, seeded, where_ref, *refs):
    pieces, refs = refs[: len(chunks)], refs[len(chunks) :]
    weights, refs = refs[:2], refs[2:]
    count = 2 * len(sets)
    seeds, outs = (refs[:count], refs[count:]) if seeded else (None, refs)
    width = outs[0].shape[1]
    for place, slot in enumerate(sets):
        for half in range(2):
            at = pl.ds(pl.multiple_of(where_ref[2 + half] * width, 128), width)
            out_ref = outs[2 * place + half]

            for side, weight in enumerate(weights):

                @pl.when(where_ref[slot] == side)
                def _(weight=weight, at=at, out_ref=out_ref, number=2 * place + half):
                    total = None
                    for (start, stop), piece in zip(chunks, pieces):
                        for part in range(3):
                            term = lax.dot_general(
                                piece[part], weight[part, at, start:stop], NT, preferred_element_type=F32
                            )
                            total = term if total is None else total + term
                    if seeded:
                        total = total + seeds[number][...]
                    out_ref[...] = total.astype(out_ref.dtype)


def back(where, pieces, chunks, weights, sets, dtypes, seeds=()):
    length = pieces[0].shape[1]
    width = weights[0].shape[2]
    depth = sum(stop - start for start, stop in chunks)
    count = 2 * len(sets)
    return pl.pallas_call(
        functools.partial(back_body, chunks, sets, bool(seeds)),
        out_shape=tuple(jax.ShapeDtypeStruct((length, width), dtypes[i // 2]) for i in range(count)),
        in_specs=[SMEM] + [VMEM] * (len(pieces) + 2 + len(seeds)),
        out_specs=(VMEM,) * count,
        compiler_params=pltpu.CompilerParams(vmem_limit_bytes=LIMIT),
        cost_estimate=cost(6 * length * count * width * depth, 6 * length * depth + 4 * count * length * width),
        name="back",
    )(where, *pieces, *weights, *seeds)


def on_device(checkpoint, projection, ctx_grad, slopes):
    dp = lax.axis_index("dp")
    tensor = lax.axis_index("tensor")
    core = dp & 1
    column_low = (tensor >> 1) & 1
    own_half = tensor & 1
    root = is_root(dp, tensor)
    side = jnp.where(root, column_low, 1 - column_low) ^ core
    where = jnp.stack([side, 1 - side, own_half, 1 - own_half]).astype(jnp.int32)

    heads = slopes.shape[0]
    size = ctx_grad.shape[3] // heads
    early = heads // 2
    columns = (early * size, (heads - early) * size)
    chunks = ((0, columns[0]), (columns[0], heads * size))

    after = lax.optimization_barrier
    own = checkpoint[0, 0]
    mine = jnp.transpose(projection[0], (1, 0, 2))
    theirs = exchange("theirs", mine, 1, 0)
    across = exchange("across", own, 0, 6)
    same = exchange("same", own, 0, 1, True)
    passed1 = jnp.where(root, across, own)
    passed2 = exchange("passed2", passed1, 0, 2)
    near1 = exchange("near1", passed1, 2, 0)
    far1 = exchange("far1", passed1, 2, 1)
    passed2, across, same, own = after((passed2, across, same, own))
    own1 = jnp.where(root, own, across)

    near2 = exchange("near2", passed2, 2, 0)
    far2 = exchange("far2", passed2, 2, 1)
    own2 = exchange("own2", own1, 0, 2)
    same1 = jnp.where(root, same, exchange("same1", same, 0, 6, True))
    weights = hold(passed2, mine, theirs)
    sums = [project(where, (near1, far1), weights, chunk, 0, F32) for chunk in chunks]
    same1, own2 = after((same1, own2))
    same2 = exchange("same2", same1, 0, 2)

    other = []
    for i in range(2):
        sent = project(where, (near2, far2), weights, chunks[i], 1, BF, sums[i])
        other.append(exchange(f"other{i}", sent, 2, 0))
    kept = [project(where, (own1, same1), weights, chunk, 0, F32) for chunk in chunks]
    kept = [project(where, (own2, same2), weights, chunks[i], 1, F32, kept[i]) for i in range(2)]
    grads = ctx_grad[0, 0]
    dqkv = [attend(slopes, kept[0], other[0], grads, 0, size)]
    other[1], ready = after((other[1], dqkv[0]))
    dqkv_other = [exchange("dqkv0", ready, 2, 0)]
    dqkv.append(attend(slopes, kept[1], other[1], grads, early, size))
    dqkv_other.append(exchange("dqkv1", dqkv[1], 2, 0))

    dqkv, first_arrived = after((dqkv, dqkv_other[0]))
    (sent0, sent1) = back(where, dqkv, chunks, weights, (1,), (BF,))
    swap1 = exchange("own_swap1", sent1, 0, 2)
    total = back(where, dqkv, chunks, weights, (0,), (F32,))
    seeds = back(where, (first_arrived,), chunks[:1], weights, (1, 0), (F32, F32))

    swap0 = exchange("own_swap0", sent0, 0, 2)
    total1 = total[1] + swap1.astype(F32)
    total0 = total[0] + swap0.astype(F32)
    dqkv_other[1], _ = after((dqkv_other[1], total))
    across1 = exchange("own_across1", total1.astype(BF), 0, 6, False)
    across0 = exchange("own_across0", total0.astype(BF), 0, 6, False)
    total1 = (total1 + across1.astype(F32)).astype(BF)
    far = exchange("own_far", total1, 0, 1, True)
    result_root = total0 + across0.astype(F32) + far.astype(F32)

    second = back(where, dqkv_other[1:], chunks[1:], weights, (1,), (BF,), seeds[:2])
    second, seeds = after((second, seeds))
    second = [exchange("second_near", second[0], 2, 0), exchange("second_far", second[1], 2, 1)]
    first = back(where, dqkv_other[1:], chunks[1:], weights, (0,), (BF,), seeds[2:])
    second[0], first = after((second[0], first))
    first = [exchange("first_near", first[0], 2, 0), exchange("first_far", first[1], 2, 1)]
    second = second[0].astype(F32) + second[1].astype(F32)
    swapped = exchange("swap", second.astype(BF), 0, 2)
    total = first[0].astype(F32) + first[1].astype(F32) + swapped.astype(F32)
    result = jnp.where(root, result_root, total).astype(BF)
    return (shift("shift", result) + shift("shift_across", total.astype(BF), 6, True))[None, None]


def solution(mesh):
    placed = (
        P("pipe", "dp", None, "tensor"),
        P("pipe", "dp", None, "tensor"),
        P("pipe", "dp", None, "tensor"),
        P("tensor"),
    )
    return jax.shard_map(
        on_device,
        mesh=mesh,
        in_specs=placed,
        out_specs=P("pipe", "dp", None, "tensor"),
        check_vma=False,
    )
```

```python
import functools

import jax
import jax.numpy as jnp
from jax import lax
from jax.experimental import pallas as pl
from jax.experimental.pallas import tpu as pltpu
from jax.sharding import PartitionSpec as P

F32 = jnp.float32
BF = jnp.bfloat16
VMEM = pl.BlockSpec(memory_space=pltpu.VMEM)
SMEM = pl.BlockSpec(memory_space=pltpu.SMEM)
NT = (((1,), (1,)), ((), ()))
TN = (((0,), (0,)), ((), ()))
LIMIT = 20 * 1024 * 1024


def cost(flops, size):
    return pl.CostEstimate(flops=flops // 20, bytes_accessed=size // 20, transcendentals=0)


def is_root(dp, tensor):
    return (tensor >> 2) == (dp >> 1)


def exchange(name, value, dp_flip, tensor_flip, senders=None):
    pairs = []
    for dp in range(4):
        for tensor in range(8):
            if senders is None or is_root(dp, tensor) == senders:
                pairs.append((dp * 8 + tensor, (dp ^ dp_flip) * 8 + (tensor ^ tensor_flip)))
    with jax.named_scope(name):
        return lax.ppermute(value, ("dp", "tensor"), pairs)


def shift(name, value, tensor_flip=0, senders=None):
    pipe = lax.axis_size("pipe")
    pairs = []
    for stage in range(pipe):
        for dp in range(4):
            for tensor in range(8):
                if senders is None or is_root(dp, tensor) == senders:
                    target = (dp * pipe + (stage - 1) % pipe) * 8 + (tensor ^ tensor_flip)
                    pairs.append(((dp * pipe + stage) * 8 + tensor, target))
    with jax.named_scope(name):
        return lax.ppermute(value, ("dp", "pipe", "tensor"), pairs)


def hold_body(after_ref, mine_ref, theirs_ref, *refs):
    del after_ref
    outs, sems = refs[:2], refs[2]
    copies = [
        pltpu.make_async_copy(source, target, sems.at[place])
        for place, (source, target) in enumerate(zip((mine_ref, theirs_ref), outs))
    ]
    for copy in copies:
        copy.start()
    for copy in copies:
        copy.wait()


def hold(after, mine, theirs):
    hbm = pl.BlockSpec(memory_space=pltpu.HBM)
    held = pl.pallas_call(
        hold_body,
        out_shape=(pltpu.VMEM(mine.shape, mine.dtype),) * 2,
        in_specs=[pl.BlockSpec(memory_space=pl.ANY), hbm, hbm],
        out_specs=(VMEM,) * 2,
        scratch_shapes=[pltpu.SemaphoreType.DMA((2,))],
        compiler_params=pltpu.CompilerParams(vmem_limit_bytes=LIMIT),
        cost_estimate=cost(0, 8 * mine.size),
        name="hold",
    )(
        after,
        pltpu.with_memory_space_constraint(mine, pltpu.HBM),
        pltpu.with_memory_space_constraint(theirs, pltpu.HBM),
    )
    return tuple(pltpu.with_memory_space_constraint(value, pltpu.VMEM) for value in held)


def project_body(columns, slot, seeded, where_ref, near_ref, far_ref, mine_ref, theirs_ref, *refs):
    width = near_ref.shape[1]
    seed_ref, out_ref, rows_ref = (refs[0] if seeded else None), refs[-2], refs[-1]
    for place, ref in enumerate((near_ref, far_ref)):
        half = where_ref[2 + place]
        rows_ref[:, pl.ds(pl.multiple_of(half * width, 128), width)] = ref[...]
    for side, weight in enumerate((mine_ref, theirs_ref)):

        @pl.when(where_ref[slot] == side)
        def _(weight=weight):
            for part in range(3):
                total = jnp.dot(rows_ref[...], weight[part, :, slice(*columns)], preferred_element_type=F32)
                if seeded:
                    total = total + seed_ref[part]
                out_ref[part] = total.astype(out_ref.dtype)


def project(where, blocks, weights, columns, slot, dtype, seed=None):
    length, width = blocks[0].shape
    some = columns[1] - columns[0]
    seeds = () if seed is None else (seed,)
    return pl.pallas_call(
        functools.partial(project_body, columns, slot, bool(seeds)),
        out_shape=jax.ShapeDtypeStruct((3, length, some), dtype),
        in_specs=[SMEM] + [VMEM] * (4 + len(seeds)),
        out_specs=VMEM,
        scratch_shapes=[pltpu.VMEM((length, 2 * width), BF)],
        compiler_params=pltpu.CompilerParams(vmem_limit_bytes=LIMIT),
        cost_estimate=cost(12 * length * width * some, 12 * length * some),
        name="project",
    )(where, *blocks, *weights, *seeds)


def attend_body(first, scale, slopes_ref, mine_ref, theirs_ref, ctx_ref, out_ref):
    length = mine_ref.shape[1]
    slope = slopes_ref[first + pl.program_id(0)]
    query, keys, values = (
        (mine_ref[part] + theirs_ref[part].astype(F32)).astype(BF) for part in range(3)
    )
    grads = ctx_ref[...]
    rows = lax.broadcasted_iota(jnp.int32, (length, length), 0)
    cols = lax.broadcasted_iota(jnp.int32, (length, length), 1)
    dist = (rows - cols).astype(F32)
    causal = rows >= cols
    scores = lax.dot_general(query, keys, NT, preferred_element_type=F32) * scale - slope * dist
    scores = jnp.where(causal, scores, -1e30)
    top = jnp.max(scores, axis=-1, keepdims=True)
    expo = jnp.where(causal, jnp.exp(scores - top), 0.0)
    probs = expo / jnp.sum(expo, axis=-1, keepdims=True)
    dprobs = lax.dot_general(grads, values, NT, preferred_element_type=F32)
    delta = jnp.sum(probs * dprobs, axis=-1, keepdims=True)
    dscore = (probs * (dprobs - delta) * scale).astype(BF)
    out_ref[0] = jnp.dot(dscore, keys, preferred_element_type=F32).astype(BF)
    out_ref[1] = lax.dot_general(dscore, query, TN, preferred_element_type=F32).astype(BF)
    out_ref[2] = lax.dot_general(probs.astype(BF), grads, TN, preferred_element_type=F32).astype(BF)


def attend(slopes, mine, theirs, ctx_grad, first, size):
    parts, length, width = mine.shape
    three = pl.BlockSpec((3, length, size), lambda head: (0, 0, head))
    return pl.pallas_call(
        functools.partial(attend_body, first, size ** (-0.5)),
        out_shape=jax.ShapeDtypeStruct((parts, length, width), BF),
        grid=(width // size,),
        in_specs=[SMEM, three, three, pl.BlockSpec((length, size), lambda head: (0, first + head))],
        out_specs=three,
        compiler_params=pltpu.CompilerParams(vmem_limit_bytes=LIMIT),
        cost_estimate=cost(10 * length * length * width, 14 * length * width),
        name="attend",
    )(slopes, mine, theirs, ctx_grad)


def back_body(chunks, sets, seeded, where_ref, *refs):
    pieces, refs = refs[: len(chunks)], refs[len(chunks) :]
    weights, refs = refs[:2], refs[2:]
    count = 2 * len(sets)
    seeds, outs = (refs[:count], refs[count:]) if seeded else (None, refs)
    width = outs[0].shape[1]
    for place, slot in enumerate(sets):
        for half in range(2):
            at = pl.ds(pl.multiple_of(where_ref[2 + half] * width, 128), width)
            out_ref = outs[2 * place + half]

            for side, weight in enumerate(weights):

                @pl.when(where_ref[slot] == side)
                def _(weight=weight, at=at, out_ref=out_ref, number=2 * place + half):
                    total = None
                    for (start, stop), piece in zip(chunks, pieces):
                        for part in range(3):
                            term = lax.dot_general(
                                piece[part], weight[part, at, start:stop], NT, preferred_element_type=F32
                            )
                            total = term if total is None else total + term
                    if seeded:
                        total = total + seeds[number][...]
                    out_ref[...] = total.astype(out_ref.dtype)


def back(where, pieces, chunks, weights, sets, dtypes, seeds=()):
    length = pieces[0].shape[1]
    width = weights[0].shape[2]
    depth = sum(stop - start for start, stop in chunks)
    count = 2 * len(sets)
    return pl.pallas_call(
        functools.partial(back_body, chunks, sets, bool(seeds)),
        out_shape=tuple(jax.ShapeDtypeStruct((length, width), dtypes[i // 2]) for i in range(count)),
        in_specs=[SMEM] + [VMEM] * (len(pieces) + 2 + len(seeds)),
        out_specs=(VMEM,) * count,
        compiler_params=pltpu.CompilerParams(vmem_limit_bytes=LIMIT),
        cost_estimate=cost(6 * length * count * width * depth, 6 * length * depth + 4 * count * length * width),
        name="back",
    )(where, *pieces, *weights, *seeds)


def on_device(checkpoint, projection, ctx_grad, slopes):
    dp = lax.axis_index("dp")
    tensor = lax.axis_index("tensor")
    core = dp & 1
    column_low = (tensor >> 1) & 1
    own_half = tensor & 1
    root = is_root(dp, tensor)
    side = jnp.where(root, column_low, 1 - column_low) ^ core
    where = jnp.stack([side, 1 - side, own_half, 1 - own_half]).astype(jnp.int32)

    heads = slopes.shape[0]
    size = ctx_grad.shape[3] // heads
    early = heads // 2
    columns = (early * size, (heads - early) * size)
    chunks = ((0, columns[0]), (columns[0], heads * size))

    after = lax.optimization_barrier
    own = checkpoint[0, 0]
    mine = jnp.transpose(projection[0], (1, 0, 2))
    theirs = exchange("theirs", mine, 1, 0)
    across = exchange("across", own, 0, 6)
    same = exchange("same", own, 0, 1, True)
    passed1 = jnp.where(root, across, own)
    passed2 = exchange("passed2", passed1, 0, 2)
    near1 = exchange("near1", passed1, 2, 0)
    far1 = exchange("far1", passed1, 2, 1)
    passed2, across, same, own = after((passed2, across, same, own))
    own1 = jnp.where(root, own, across)

    near2 = exchange("near2", passed2, 2, 0)
    far2 = exchange("far2", passed2, 2, 1)
    weights = hold(passed2, mine, theirs)
    sums = [project(where, (near1, far1), weights, chunk, 0, F32) for chunk in chunks]
    sums[0], own1, same = after((sums[0], own1, same))
    own2 = exchange("own2", own1, 0, 2)
    same1 = jnp.where(root, same, exchange("same1", same, 0, 6, True))
    same1, own2 = after((same1, own2))
    same2 = exchange("same2", same1, 0, 2)

    other = []
    for i in range(2):
        sent = project(where, (near2, far2), weights, chunks[i], 1, BF, sums[i])
        other.append(exchange(f"other{i}", sent, 2, 0))
    kept = [project(where, (own1, same1), weights, chunk, 0, F32) for chunk in chunks]
    kept = [project(where, (own2, same2), weights, chunks[i], 1, F32, kept[i]) for i in range(2)]
    grads = ctx_grad[0, 0]
    dqkv = [attend(slopes, kept[0], other[0], grads, 0, size)]
    partial = back(where, dqkv, chunks[:1], weights, (1,), (F32,))
    other[1], ready, kept[1], partial = after((other[1], dqkv[0], kept[1], partial))
    dqkv_other = [exchange("dqkv0", ready, 2, 0)]
    dqkv.append(attend(slopes, kept[1], other[1], grads, early, size))
    dqkv_other.append(exchange("dqkv1", dqkv[1], 2, 0))

    dqkv, first_arrived = after((dqkv, dqkv_other[0]))
    (sent0, sent1) = back(where, dqkv[1:], chunks[1:], weights, (1,), (BF,), partial)
    swap1 = exchange("own_swap1", sent1, 0, 2)
    swap0 = exchange("own_swap0", sent0, 0, 2)
    total = back(where, dqkv, chunks, weights, (0,), (F32,))
    seeds = back(where, (first_arrived,), chunks[:1], weights, (1, 0), (F32, F32))
    total1 = total[1] + swap1.astype(F32)
    total0 = total[0] + swap0.astype(F32)
    dqkv_other[1], _ = after((dqkv_other[1], total))
    across1 = exchange("own_across1", total1.astype(BF), 0, 6, False)
    across0 = exchange("own_across0", total0.astype(BF), 0, 6, False)
    total1 = (total1 + across1.astype(F32)).astype(BF)
    far = exchange("own_far", total1, 0, 1, True)
    result_root = total0 + across0.astype(F32) + far.astype(F32)

    second = back(where, dqkv_other[1:], chunks[1:], weights, (1,), (BF,), seeds[:2])
    second, seeds = after((second, seeds))
    second = [exchange("second_near", second[0], 2, 0), exchange("second_far", second[1], 2, 1)]
    first = back(where, dqkv_other[1:], chunks[1:], weights, (0,), (BF,), seeds[2:])
    second[0], first = after((second[0], first))
    first = [exchange("first_near", first[0], 2, 0), exchange("first_far", first[1], 2, 1)]
    second = second[0].astype(F32) + second[1].astype(F32)
    swapped = exchange("swap", second.astype(BF), 0, 2)
    total = first[0].astype(F32) + first[1].astype(F32) + swapped.astype(F32)
    result = jnp.where(root, result_root, total).astype(BF)
    return (shift("shift", result) + shift("shift_across", total.astype(BF), 6, True))[None, None]


def solution(mesh):
    placed = (
        P("pipe", "dp", None, "tensor"),
        P("pipe", "dp", None, "tensor"),
        P("pipe", "dp", None, "tensor"),
        P("tensor"),
    )
    return jax.shard_map(
        on_device,
        mesh=mesh,
        in_specs=placed,
        out_specs=P("pipe", "dp", None, "tensor"),
        check_vma=False,
    )
```

```python
import functools

import jax
import jax.numpy as jnp
from jax import lax
from jax.experimental import pallas as pl
from jax.experimental.pallas import tpu as pltpu
from jax.sharding import PartitionSpec as P

F32 = jnp.float32
BF = jnp.bfloat16
VMEM = pl.BlockSpec(memory_space=pltpu.VMEM)
SMEM = pl.BlockSpec(memory_space=pltpu.SMEM)
NT = (((1,), (1,)), ((), ()))
TN = (((0,), (0,)), ((), ()))
LIMIT = 20 * 1024 * 1024


def cost(flops, size):
    return pl.CostEstimate(flops=flops // 20, bytes_accessed=size // 20, transcendentals=0)


def is_root(dp, tensor):
    return (tensor >> 2) == (dp >> 1)


def exchange(name, value, dp_flip, tensor_flip, senders=None):
    pairs = []
    for dp in range(4):
        for tensor in range(8):
            if senders is None or is_root(dp, tensor) == senders:
                pairs.append((dp * 8 + tensor, (dp ^ dp_flip) * 8 + (tensor ^ tensor_flip)))
    with jax.named_scope(name):
        return lax.ppermute(value, ("dp", "tensor"), pairs)


def shift(name, value, tensor_flip=0, senders=None):
    pipe = lax.axis_size("pipe")
    pairs = []
    for stage in range(pipe):
        for dp in range(4):
            for tensor in range(8):
                if senders is None or is_root(dp, tensor) == senders:
                    target = (dp * pipe + (stage - 1) % pipe) * 8 + (tensor ^ tensor_flip)
                    pairs.append(((dp * pipe + stage) * 8 + tensor, target))
    with jax.named_scope(name):
        return lax.ppermute(value, ("dp", "pipe", "tensor"), pairs)


def hold_body(after_ref, mine_ref, theirs_ref, *refs):
    del after_ref
    outs, sems = refs[:2], refs[2]
    copies = [
        pltpu.make_async_copy(source, target, sems.at[place])
        for place, (source, target) in enumerate(zip((mine_ref, theirs_ref), outs))
    ]
    for copy in copies:
        copy.start()
    for copy in copies:
        copy.wait()


def hold(after, mine, theirs):
    hbm = pl.BlockSpec(memory_space=pltpu.HBM)
    held = pl.pallas_call(
        hold_body,
        out_shape=(pltpu.VMEM(mine.shape, mine.dtype),) * 2,
        in_specs=[pl.BlockSpec(memory_space=pl.ANY), hbm, hbm],
        out_specs=(VMEM,) * 2,
        scratch_shapes=[pltpu.SemaphoreType.DMA((2,))],
        compiler_params=pltpu.CompilerParams(vmem_limit_bytes=LIMIT),
        cost_estimate=cost(0, 8 * mine.size),
        name="hold",
    )(
        after,
        pltpu.with_memory_space_constraint(mine, pltpu.HBM),
        pltpu.with_memory_space_constraint(theirs, pltpu.HBM),
    )
    return tuple(pltpu.with_memory_space_constraint(value, pltpu.VMEM) for value in held)


def project_body(columns, slot, seeded, where_ref, near_ref, far_ref, mine_ref, theirs_ref, *refs):
    width = near_ref.shape[1]
    seed_ref, out_ref, rows_ref = (refs[0] if seeded else None), refs[-2], refs[-1]
    for place, ref in enumerate((near_ref, far_ref)):
        half = where_ref[2 + place]
        rows_ref[:, pl.ds(pl.multiple_of(half * width, 128), width)] = ref[...]
    for side, weight in enumerate((mine_ref, theirs_ref)):

        @pl.when(where_ref[slot] == side)
        def _(weight=weight):
            for part in range(3):
                total = jnp.dot(rows_ref[...], weight[part, :, slice(*columns)], preferred_element_type=F32)
                if seeded:
                    total = total + seed_ref[part]
                out_ref[part] = total.astype(out_ref.dtype)


def project(where, blocks, weights, columns, slot, dtype, seed=None):
    length, width = blocks[0].shape
    some = columns[1] - columns[0]
    seeds = () if seed is None else (seed,)
    return pl.pallas_call(
        functools.partial(project_body, columns, slot, bool(seeds)),
        out_shape=jax.ShapeDtypeStruct((3, length, some), dtype),
        in_specs=[SMEM] + [VMEM] * (4 + len(seeds)),
        out_specs=VMEM,
        scratch_shapes=[pltpu.VMEM((length, 2 * width), BF)],
        compiler_params=pltpu.CompilerParams(vmem_limit_bytes=LIMIT),
        cost_estimate=cost(12 * length * width * some, 12 * length * some),
        name="project",
    )(where, *blocks, *weights, *seeds)


def attend_body(first, scale, slopes_ref, mine_ref, theirs_ref, ctx_ref, out_ref):
    length = mine_ref.shape[1]
    slope = slopes_ref[first + pl.program_id(0)]
    query, keys, values = (
        (mine_ref[part] + theirs_ref[part].astype(F32)).astype(BF) for part in range(3)
    )
    grads = ctx_ref[...]
    rows = lax.broadcasted_iota(jnp.int32, (length, length), 0)
    cols = lax.broadcasted_iota(jnp.int32, (length, length), 1)
    dist = (rows - cols).astype(F32)
    causal = rows >= cols
    scores = lax.dot_general(query, keys, NT, preferred_element_type=F32) * scale - slope * dist
    scores = jnp.where(causal, scores, -1e30)
    top = jnp.max(scores, axis=-1, keepdims=True)
    expo = jnp.where(causal, jnp.exp(scores - top), 0.0)
    probs = expo / jnp.sum(expo, axis=-1, keepdims=True)
    dprobs = lax.dot_general(grads, values, NT, preferred_element_type=F32)
    delta = jnp.sum(probs * dprobs, axis=-1, keepdims=True)
    dscore = (probs * (dprobs - delta) * scale).astype(BF)
    out_ref[0] = jnp.dot(dscore, keys, preferred_element_type=F32).astype(BF)
    out_ref[1] = lax.dot_general(dscore, query, TN, preferred_element_type=F32).astype(BF)
    out_ref[2] = lax.dot_general(probs.astype(BF), grads, TN, preferred_element_type=F32).astype(BF)


def attend(slopes, mine, theirs, ctx_grad, first, size):
    parts, length, width = mine.shape
    three = pl.BlockSpec((3, length, size), lambda head: (0, 0, head))
    return pl.pallas_call(
        functools.partial(attend_body, first, size ** (-0.5)),
        out_shape=jax.ShapeDtypeStruct((parts, length, width), BF),
        grid=(width // size,),
        in_specs=[SMEM, three, three, pl.BlockSpec((length, size), lambda head: (0, first + head))],
        out_specs=three,
        compiler_params=pltpu.CompilerParams(vmem_limit_bytes=LIMIT),
        cost_estimate=cost(10 * length * length * width, 14 * length * width),
        name="attend",
    )(slopes, mine, theirs, ctx_grad)


def back_body(chunks, sets, seeded, where_ref, *refs):
    pieces, refs = refs[: len(chunks)], refs[len(chunks) :]
    weights, refs = refs[:2], refs[2:]
    count = 2 * len(sets)
    seeds, outs = (refs[:count], refs[count:]) if seeded else (None, refs)
    width = outs[0].shape[1]
    for place, slot in enumerate(sets):
        for half in range(2):
            at = pl.ds(pl.multiple_of(where_ref[2 + half] * width, 128), width)
            out_ref = outs[2 * place + half]

            for side, weight in enumerate(weights):

                @pl.when(where_ref[slot] == side)
                def _(weight=weight, at=at, out_ref=out_ref, number=2 * place + half):
                    total = None
                    for (start, stop), piece in zip(chunks, pieces):
                        for part in range(3):
                            term = lax.dot_general(
                                piece[part], weight[part, at, start:stop], NT, preferred_element_type=F32
                            )
                            total = term if total is None else total + term
                    if seeded:
                        total = total + seeds[number][...]
                    out_ref[...] = total.astype(out_ref.dtype)


def back(where, pieces, chunks, weights, sets, dtypes, seeds=()):
    length = pieces[0].shape[1]
    width = weights[0].shape[2]
    depth = sum(stop - start for start, stop in chunks)
    count = 2 * len(sets)
    return pl.pallas_call(
        functools.partial(back_body, chunks, sets, bool(seeds)),
        out_shape=tuple(jax.ShapeDtypeStruct((length, width), dtypes[i // 2]) for i in range(count)),
        in_specs=[SMEM] + [VMEM] * (len(pieces) + 2 + len(seeds)),
        out_specs=(VMEM,) * count,
        compiler_params=pltpu.CompilerParams(vmem_limit_bytes=LIMIT),
        cost_estimate=cost(6 * length * count * width * depth, 6 * length * depth + 4 * count * length * width),
        name="back",
    )(where, *pieces, *weights, *seeds)


def on_device(checkpoint, projection, ctx_grad, slopes):
    dp = lax.axis_index("dp")
    tensor = lax.axis_index("tensor")
    core = dp & 1
    column_low = (tensor >> 1) & 1
    own_half = tensor & 1
    root = is_root(dp, tensor)
    side = jnp.where(root, column_low, 1 - column_low) ^ core
    where = jnp.stack([side, 1 - side, own_half, 1 - own_half]).astype(jnp.int32)

    heads = slopes.shape[0]
    size = ctx_grad.shape[3] // heads
    early = heads // 2
    columns = (early * size, (heads - early) * size)
    chunks = ((0, columns[0]), (columns[0], heads * size))

    after = lax.optimization_barrier
    own = checkpoint[0, 0]
    mine = jnp.transpose(projection[0], (1, 0, 2))
    theirs = exchange("theirs", mine, 1, 0)
    across = exchange("across", own, 0, 6)
    same = exchange("same", own, 0, 1, True)
    passed1 = jnp.where(root, across, own)
    passed2 = exchange("passed2", passed1, 0, 2)
    near1 = exchange("near1", passed1, 2, 0)
    far1 = exchange("far1", passed1, 2, 1)
    passed2, across, same, own = after((passed2, across, same, own))
    own1 = jnp.where(root, own, across)

    near2 = exchange("near2", passed2, 2, 0)
    far2 = exchange("far2", passed2, 2, 1)
    weights = hold(passed2, mine, theirs)
    sums = [project(where, (near1, far1), weights, chunk, 0, F32) for chunk in chunks]
    sums[0], own1, same = after((sums[0], own1, same))
    own2 = exchange("own2", own1, 0, 2)
    same1 = jnp.where(root, same, exchange("same1", same, 0, 6, True))
    same1, own2 = after((same1, own2))
    same2 = exchange("same2", same1, 0, 2)

    other = []
    for i in range(2):
        sent = project(where, (near2, far2), weights, chunks[i], 1, BF, sums[i])
        other.append(exchange(f"other{i}", sent, 2, 0))
    kept = [project(where, (own1, same1), weights, chunk, 0, F32) for chunk in chunks]
    kept = [project(where, (own2, same2), weights, chunks[i], 1, F32, kept[i]) for i in range(2)]
    grads = ctx_grad[0, 0]
    dqkv = [attend(slopes, kept[0], other[0], grads, 0, size)]
    partial = back(where, dqkv, chunks[:1], weights, (1,), (F32,))
    other[1], ready, kept[1], partial = after((other[1], dqkv[0], kept[1], partial))
    dqkv_other = [exchange("dqkv0", ready, 2, 0)]
    dqkv.append(attend(slopes, kept[1], other[1], grads, early, size))
    dqkv_other.append(exchange("dqkv1", dqkv[1], 2, 0))

    (sent0, sent1) = back(where, dqkv[1:], chunks[1:], weights, (1,), (BF,), partial)
    swap1 = exchange("own_swap1", sent1, 0, 2)
    swap0 = exchange("own_swap0", sent0, 0, 2)
    dqkv, first_arrived = after((dqkv, dqkv_other[0]))
    total = back(where, dqkv, chunks, weights, (0,), (F32,))
    seeds = back(where, (first_arrived,), chunks[:1], weights, (1, 0), (F32, F32))
    total1 = total[1] + swap1.astype(F32)
    total0 = total[0] + swap0.astype(F32)
    dqkv_other[1], _ = after((dqkv_other[1], total))
    second = back(where, dqkv_other[1:], chunks[1:], weights, (1,), (BF,), seeds[:2])
    second, seeds, total1, total0 = after((second, seeds, total1, total0))
    across1 = exchange("own_across1", total1.astype(BF), 0, 6, False)
    across0 = exchange("own_across0", total0.astype(BF), 0, 6, False)
    total1 = (total1 + across1.astype(F32)).astype(BF)
    far = exchange("own_far", total1, 0, 1, True)
    result_root = total0 + across0.astype(F32) + far.astype(F32)
    second = [exchange("second_near", second[0], 2, 0), exchange("second_far", second[1], 2, 1)]
    first = back(where, dqkv_other[1:], chunks[1:], weights, (0,), (BF,), seeds[2:])
    first = [exchange("first_near", first[0], 2, 0), exchange("first_far", first[1], 2, 1)]
    second = second[0].astype(F32) + second[1].astype(F32)
    swapped = exchange("swap", second.astype(BF), 0, 2)
    total = first[0].astype(F32) + first[1].astype(F32) + swapped.astype(F32)
    result = jnp.where(root, result_root, total).astype(BF)
    return (shift("shift", result) + shift("shift_across", total.astype(BF), 6, True))[None, None]


def solution(mesh):
    placed = (
        P("pipe", "dp", None, "tensor"),
        P("pipe", "dp", None, "tensor"),
        P("pipe", "dp", None, "tensor"),
        P("tensor"),
    )
    return jax.shard_map(
        on_device,
        mesh=mesh,
        in_specs=placed,
        out_specs=P("pipe", "dp", None, "tensor"),
        check_vma=False,
    )
```

```python
import functools

import jax
import jax.numpy as jnp
from jax import lax
from jax.experimental import pallas as pl
from jax.experimental.pallas import tpu as pltpu
from jax.sharding import PartitionSpec as P

F32 = jnp.float32
BF = jnp.bfloat16
VMEM = pl.BlockSpec(memory_space=pltpu.VMEM)
SMEM = pl.BlockSpec(memory_space=pltpu.SMEM)
NT = (((1,), (1,)), ((), ()))
TN = (((0,), (0,)), ((), ()))
LIMIT = 20 * 1024 * 1024


def cost(flops, size):
    return pl.CostEstimate(flops=flops // 20, bytes_accessed=size // 20, transcendentals=0)


def is_root(dp, tensor):
    return (tensor >> 2) == (dp >> 1)


def exchange(name, value, dp_flip, tensor_flip, senders=None):
    pairs = []
    for dp in range(4):
        for tensor in range(8):
            if senders is None or is_root(dp, tensor) == senders:
                pairs.append((dp * 8 + tensor, (dp ^ dp_flip) * 8 + (tensor ^ tensor_flip)))
    with jax.named_scope(name):
        return lax.ppermute(value, ("dp", "tensor"), pairs)


def shift(name, value, tensor_flip=0, senders=None):
    pipe = lax.axis_size("pipe")
    pairs = []
    for stage in range(pipe):
        for dp in range(4):
            for tensor in range(8):
                if senders is None or is_root(dp, tensor) == senders:
                    target = (dp * pipe + (stage - 1) % pipe) * 8 + (tensor ^ tensor_flip)
                    pairs.append(((dp * pipe + stage) * 8 + tensor, target))
    with jax.named_scope(name):
        return lax.ppermute(value, ("dp", "pipe", "tensor"), pairs)


def hold_body(after_ref, mine_ref, theirs_ref, *refs):
    del after_ref
    outs, sems = refs[:2], refs[2]
    copies = [
        pltpu.make_async_copy(source, target, sems.at[place])
        for place, (source, target) in enumerate(zip((mine_ref, theirs_ref), outs))
    ]
    for copy in copies:
        copy.start()
    for copy in copies:
        copy.wait()


def hold(after, mine, theirs):
    hbm = pl.BlockSpec(memory_space=pltpu.HBM)
    held = pl.pallas_call(
        hold_body,
        out_shape=(pltpu.VMEM(mine.shape, mine.dtype),) * 2,
        in_specs=[pl.BlockSpec(memory_space=pl.ANY), hbm, hbm],
        out_specs=(VMEM,) * 2,
        scratch_shapes=[pltpu.SemaphoreType.DMA((2,))],
        compiler_params=pltpu.CompilerParams(vmem_limit_bytes=LIMIT),
        cost_estimate=cost(0, 8 * mine.size),
        name="hold",
    )(
        after,
        pltpu.with_memory_space_constraint(mine, pltpu.HBM),
        pltpu.with_memory_space_constraint(theirs, pltpu.HBM),
    )
    return tuple(pltpu.with_memory_space_constraint(value, pltpu.VMEM) for value in held)


def project_body(columns, slot, seeded, where_ref, near_ref, far_ref, mine_ref, theirs_ref, *refs):
    width = near_ref.shape[1]
    seed_ref, out_ref, rows_ref = (refs[0] if seeded else None), refs[-2], refs[-1]
    for place, ref in enumerate((near_ref, far_ref)):
        half = where_ref[2 + place]
        rows_ref[:, pl.ds(pl.multiple_of(half * width, 128), width)] = ref[...]
    for side, weight in enumerate((mine_ref, theirs_ref)):

        @pl.when(where_ref[slot] == side)
        def _(weight=weight):
            for part in range(3):
                total = jnp.dot(rows_ref[...], weight[part, :, slice(*columns)], preferred_element_type=F32)
                if seeded:
                    total = total + seed_ref[part]
                out_ref[part] = total.astype(out_ref.dtype)


def project(where, blocks, weights, columns, slot, dtype, seed=None):
    length, width = blocks[0].shape
    some = columns[1] - columns[0]
    seeds = () if seed is None else (seed,)
    return pl.pallas_call(
        functools.partial(project_body, columns, slot, bool(seeds)),
        out_shape=jax.ShapeDtypeStruct((3, length, some), dtype),
        in_specs=[SMEM] + [VMEM] * (4 + len(seeds)),
        out_specs=VMEM,
        scratch_shapes=[pltpu.VMEM((length, 2 * width), BF)],
        compiler_params=pltpu.CompilerParams(vmem_limit_bytes=LIMIT),
        cost_estimate=cost(12 * length * width * some, 12 * length * some),
        name="project",
    )(where, *blocks, *weights, *seeds)


def attend_body(first, scale, slopes_ref, mine_ref, theirs_ref, ctx_ref, out_ref):
    length = mine_ref.shape[1]
    slope = slopes_ref[first + pl.program_id(0)]
    query, keys, values = (
        (mine_ref[part] + theirs_ref[part].astype(F32)).astype(BF) for part in range(3)
    )
    grads = ctx_ref[...]
    rows = lax.broadcasted_iota(jnp.int32, (length, length), 0)
    cols = lax.broadcasted_iota(jnp.int32, (length, length), 1)
    dist = (rows - cols).astype(F32)
    causal = rows >= cols
    scores = lax.dot_general(query, keys, NT, preferred_element_type=F32) * scale - slope * dist
    scores = jnp.where(causal, scores, -1e30)
    top = jnp.max(scores, axis=-1, keepdims=True)
    expo = jnp.where(causal, jnp.exp(scores - top), 0.0)
    probs = expo / jnp.sum(expo, axis=-1, keepdims=True)
    dprobs = lax.dot_general(grads, values, NT, preferred_element_type=F32)
    delta = jnp.sum(probs * dprobs, axis=-1, keepdims=True)
    dscore = (probs * (dprobs - delta) * scale).astype(BF)
    out_ref[0] = jnp.dot(dscore, keys, preferred_element_type=F32).astype(BF)
    out_ref[1] = lax.dot_general(dscore, query, TN, preferred_element_type=F32).astype(BF)
    out_ref[2] = lax.dot_general(probs.astype(BF), grads, TN, preferred_element_type=F32).astype(BF)


def attend(slopes, mine, theirs, ctx_grad, first, size):
    parts, length, width = mine.shape
    three = pl.BlockSpec((3, length, size), lambda head: (0, 0, head))
    return pl.pallas_call(
        functools.partial(attend_body, first, size ** (-0.5)),
        out_shape=jax.ShapeDtypeStruct((parts, length, width), BF),
        grid=(width // size,),
        in_specs=[SMEM, three, three, pl.BlockSpec((length, size), lambda head: (0, first + head))],
        out_specs=three,
        compiler_params=pltpu.CompilerParams(vmem_limit_bytes=LIMIT),
        cost_estimate=cost(10 * length * length * width, 14 * length * width),
        name="attend",
    )(slopes, mine, theirs, ctx_grad)


def back_body(chunks, sets, seeded, where_ref, *refs):
    pieces, refs = refs[: len(chunks)], refs[len(chunks) :]
    weights, refs = refs[:2], refs[2:]
    count = 2 * len(sets)
    seeds, outs = (refs[:count], refs[count:]) if seeded else (None, refs)
    width = outs[0].shape[1]
    for place, slot in enumerate(sets):
        for half in range(2):
            at = pl.ds(pl.multiple_of(where_ref[2 + half] * width, 128), width)
            out_ref = outs[2 * place + half]

            for side, weight in enumerate(weights):

                @pl.when(where_ref[slot] == side)
                def _(weight=weight, at=at, out_ref=out_ref, number=2 * place + half):
                    total = None
                    for (start, stop), piece in zip(chunks, pieces):
                        for part in range(3):
                            term = lax.dot_general(
                                piece[part], weight[part, at, start:stop], NT, preferred_element_type=F32
                            )
                            total = term if total is None else total + term
                    if seeded:
                        total = total + seeds[number][...]
                    out_ref[...] = total.astype(out_ref.dtype)


def back(where, pieces, chunks, weights, sets, dtypes, seeds=()):
    length = pieces[0].shape[1]
    width = weights[0].shape[2]
    depth = sum(stop - start for start, stop in chunks)
    count = 2 * len(sets)
    return pl.pallas_call(
        functools.partial(back_body, chunks, sets, bool(seeds)),
        out_shape=tuple(jax.ShapeDtypeStruct((length, width), dtypes[i // 2]) for i in range(count)),
        in_specs=[SMEM] + [VMEM] * (len(pieces) + 2 + len(seeds)),
        out_specs=(VMEM,) * count,
        compiler_params=pltpu.CompilerParams(vmem_limit_bytes=LIMIT),
        cost_estimate=cost(6 * length * count * width * depth, 6 * length * depth + 4 * count * length * width),
        name="back",
    )(where, *pieces, *weights, *seeds)


def on_device(checkpoint, projection, ctx_grad, slopes):
    dp = lax.axis_index("dp")
    tensor = lax.axis_index("tensor")
    core = dp & 1
    column_low = (tensor >> 1) & 1
    own_half = tensor & 1
    root = is_root(dp, tensor)
    side = jnp.where(root, column_low, 1 - column_low) ^ core
    where = jnp.stack([side, 1 - side, own_half, 1 - own_half]).astype(jnp.int32)

    heads = slopes.shape[0]
    size = ctx_grad.shape[3] // heads
    early = heads // 2
    columns = (early * size, (heads - early) * size)
    chunks = ((0, columns[0]), (columns[0], heads * size))

    after = lax.optimization_barrier
    own = checkpoint[0, 0]
    mine = jnp.transpose(projection[0], (1, 0, 2))
    theirs = exchange("theirs", mine, 1, 0)
    across = exchange("across", own, 0, 6)
    same = exchange("same", own, 0, 1, True)
    passed1 = jnp.where(root, across, own)
    passed2 = exchange("passed2", passed1, 0, 2)
    near1 = exchange("near1", passed1, 2, 0)
    far1 = exchange("far1", passed1, 2, 1)
    passed2, across, same, own = after((passed2, across, same, own))
    own1 = jnp.where(root, own, across)

    near2 = exchange("near2", passed2, 2, 0)
    far2 = exchange("far2", passed2, 2, 1)
    weights = hold(passed2, mine, theirs)
    sums = [project(where, (near1, far1), weights, chunk, 0, F32) for chunk in chunks]
    sums[0], own1, same = after((sums[0], own1, same))
    own2 = exchange("own2", own1, 0, 2)
    same1 = jnp.where(root, same, exchange("same1", same, 0, 6))
    same1, own2 = after((same1, own2))
    same2 = exchange("same2", same1, 0, 2)

    other = []
    for i in range(2):
        sent = project(where, (near2, far2), weights, chunks[i], 1, BF, sums[i])
        other.append(exchange(f"other{i}", sent, 2, 0))
    kept = [project(where, (own1, same1), weights, chunk, 0, F32) for chunk in chunks]
    kept = [project(where, (own2, same2), weights, chunks[i], 1, F32, kept[i]) for i in range(2)]
    grads = ctx_grad[0, 0]
    dqkv = [attend(slopes, kept[0], other[0], grads, 0, size)]
    partial = back(where, dqkv, chunks[:1], weights, (1,), (F32,))
    other[1], ready, kept[1], partial = after((other[1], dqkv[0], kept[1], partial))
    dqkv_other = [exchange("dqkv0", ready, 2, 0)]
    dqkv.append(attend(slopes, kept[1], other[1], grads, early, size))
    dqkv_other.append(exchange("dqkv1", dqkv[1], 2, 0))

    (sent0, sent1) = back(where, dqkv[1:], chunks[1:], weights, (1,), (BF,), partial)
    swap1 = exchange("own_swap1", sent1, 0, 2)
    swap0 = exchange("own_swap0", sent0, 0, 2)
    dqkv, first_arrived = after((dqkv, dqkv_other[0]))
    total = back(where, dqkv, chunks, weights, (0,), (F32,))
    seeds = back(where, (first_arrived,), chunks[:1], weights, (1, 0), (F32, F32))
    total1 = total[1] + swap1.astype(F32)
    total0 = total[0] + swap0.astype(F32)
    dqkv_other[1], _ = after((dqkv_other[1], total))
    second = back(where, dqkv_other[1:], chunks[1:], weights, (1,), (BF,), seeds[:2])
    second, seeds, total1, total0 = after((second, seeds, total1, total0))
    across1 = exchange("own_across1", total1.astype(BF), 0, 6)
    across0 = exchange("own_across0", total0.astype(BF), 0, 6)
    total1 = (total1 + across1.astype(F32)).astype(BF)
    far = exchange("own_far", total1, 0, 1, True)
    result_root = total0 + across0.astype(F32) + far.astype(F32)
    second = [exchange("second_near", second[0], 2, 0), exchange("second_far", second[1], 2, 1)]
    first = back(where, dqkv_other[1:], chunks[1:], weights, (0,), (BF,), seeds[2:])
    first = [exchange("first_near", first[0], 2, 0), exchange("first_far", first[1], 2, 1)]
    second = second[0].astype(F32) + second[1].astype(F32)
    swapped = exchange("swap", second.astype(BF), 0, 2)
    total = first[0].astype(F32) + first[1].astype(F32) + swapped.astype(F32)
    result = jnp.where(root, result_root, total).astype(BF)
    return (shift("shift", result) + shift("shift_across", total.astype(BF), 6, True))[None, None]


def solution(mesh):
    placed = (
        P("pipe", "dp", None, "tensor"),
        P("pipe", "dp", None, "tensor"),
        P("pipe", "dp", None, "tensor"),
        P("tensor"),
    )
    return jax.shard_map(
        on_device,
        mesh=mesh,
        in_specs=placed,
        out_specs=P("pipe", "dp", None, "tensor"),
        check_vma=False,
    )
```

```python
import functools

import jax
import jax.numpy as jnp
from jax import lax
from jax.experimental import pallas as pl
from jax.experimental.pallas import tpu as pltpu
from jax.sharding import PartitionSpec as P

F32 = jnp.float32
BF = jnp.bfloat16
VMEM = pl.BlockSpec(memory_space=pltpu.VMEM)
SMEM = pl.BlockSpec(memory_space=pltpu.SMEM)
NT = (((1,), (1,)), ((), ()))
TN = (((0,), (0,)), ((), ()))
LIMIT = 20 * 1024 * 1024


def cost(flops, size):
    return pl.CostEstimate(flops=flops // 20, bytes_accessed=size // 20, transcendentals=0)


def is_root(dp, tensor):
    return (tensor >> 2) == (dp >> 1)


def exchange(name, value, dp_flip, tensor_flip, senders=None):
    pairs = []
    for dp in range(4):
        for tensor in range(8):
            if senders is None or is_root(dp, tensor) == senders:
                pairs.append((dp * 8 + tensor, (dp ^ dp_flip) * 8 + (tensor ^ tensor_flip)))
    with jax.named_scope(name):
        return lax.ppermute(value, ("dp", "tensor"), pairs)


def shift(name, value, tensor_flip=0, senders=None):
    pipe = lax.axis_size("pipe")
    pairs = []
    for stage in range(pipe):
        for dp in range(4):
            for tensor in range(8):
                if senders is None or is_root(dp, tensor) == senders:
                    target = (dp * pipe + (stage - 1) % pipe) * 8 + (tensor ^ tensor_flip)
                    pairs.append(((dp * pipe + stage) * 8 + tensor, target))
    with jax.named_scope(name):
        return lax.ppermute(value, ("dp", "pipe", "tensor"), pairs)


def hold_body(columns, slot, after_ref, where_ref, near_ref, far_ref, mine_ref, theirs_ref, *refs):
    del after_ref
    held, out_refs, (rows_ref, sems) = refs[:2], refs[2:-2], refs[-2:]
    copies = [
        [
            pltpu.make_async_copy(source.at[part], target.at[part], sems.at[side, part])
            for side, (source, target) in enumerate(zip((mine_ref, theirs_ref), held))
        ]
        for part in range(3)
    ]
    for pair in copies:
        for copy in pair:
            copy.start()
    width = near_ref.shape[1]
    for place, ref in enumerate((near_ref, far_ref)):
        half = where_ref[2 + place]
        rows_ref[:, pl.ds(pl.multiple_of(half * width, 128), width)] = ref[...]
    for part, pair in enumerate(copies):
        for copy in pair:
            copy.wait()
        for side, weight in enumerate(held):

            @pl.when(where_ref[slot] == side)
            def _(weight=weight, part=part):
                for some, out_ref in zip(columns, out_refs):
                    out_ref[part] = jnp.dot(
                        rows_ref[...], weight[part, :, slice(*some)], preferred_element_type=F32
                    )


def hold(after, where, blocks, mine, theirs, columns, slot):
    hbm = pl.BlockSpec(memory_space=pltpu.HBM)
    length, width = blocks[0].shape
    mine_held, theirs_held, *sums = pl.pallas_call(
        functools.partial(hold_body, columns, slot),
        out_shape=(pltpu.VMEM(mine.shape, mine.dtype),) * 2
        + tuple(jax.ShapeDtypeStruct((3, length, stop - start), F32) for start, stop in columns),
        in_specs=[pl.BlockSpec(memory_space=pl.ANY), SMEM, VMEM, VMEM, hbm, hbm],
        out_specs=(VMEM,) * (2 + len(columns)),
        scratch_shapes=[pltpu.VMEM((length, 2 * width), BF), pltpu.SemaphoreType.DMA((2, 3))],
        compiler_params=pltpu.CompilerParams(vmem_limit_bytes=LIMIT),
        cost_estimate=cost(12 * length * width * 3 * width, 8 * mine.size),
        name="hold",
    )(
        after,
        where,
        *blocks,
        pltpu.with_memory_space_constraint(mine, pltpu.HBM),
        pltpu.with_memory_space_constraint(theirs, pltpu.HBM),
    )
    weights = tuple(
        pltpu.with_memory_space_constraint(value, pltpu.VMEM) for value in (mine_held, theirs_held)
    )
    return weights, sums


def project_body(columns, slot, seeded, where_ref, near_ref, far_ref, mine_ref, theirs_ref, *refs):
    width = near_ref.shape[1]
    seed_ref, out_ref, rows_ref = (refs[0] if seeded else None), refs[-2], refs[-1]
    for place, ref in enumerate((near_ref, far_ref)):
        half = where_ref[2 + place]
        rows_ref[:, pl.ds(pl.multiple_of(half * width, 128), width)] = ref[...]
    for side, weight in enumerate((mine_ref, theirs_ref)):

        @pl.when(where_ref[slot] == side)
        def _(weight=weight):
            for part in range(3):
                total = jnp.dot(rows_ref[...], weight[part, :, slice(*columns)], preferred_element_type=F32)
                if seeded:
                    total = total + seed_ref[part]
                out_ref[part] = total.astype(out_ref.dtype)


def project(where, blocks, weights, columns, slot, dtype, seed=None):
    length, width = blocks[0].shape
    some = columns[1] - columns[0]
    seeds = () if seed is None else (seed,)
    return pl.pallas_call(
        functools.partial(project_body, columns, slot, bool(seeds)),
        out_shape=jax.ShapeDtypeStruct((3, length, some), dtype),
        in_specs=[SMEM] + [VMEM] * (4 + len(seeds)),
        out_specs=VMEM,
        scratch_shapes=[pltpu.VMEM((length, 2 * width), BF)],
        compiler_params=pltpu.CompilerParams(vmem_limit_bytes=LIMIT),
        cost_estimate=cost(12 * length * width * some, 12 * length * some),
        name="project",
    )(where, *blocks, *weights, *seeds)


def attend_body(first, scale, slopes_ref, mine_ref, theirs_ref, ctx_ref, out_ref):
    length = mine_ref.shape[1]
    slope = slopes_ref[first + pl.program_id(0)]
    query, keys, values = (
        (mine_ref[part] + theirs_ref[part].astype(F32)).astype(BF) for part in range(3)
    )
    grads = ctx_ref[...]
    rows = lax.broadcasted_iota(jnp.int32, (length, length), 0)
    cols = lax.broadcasted_iota(jnp.int32, (length, length), 1)
    dist = (rows - cols).astype(F32)
    causal = rows >= cols
    scores = lax.dot_general(query, keys, NT, preferred_element_type=F32) * scale - slope * dist
    scores = jnp.where(causal, scores, -1e30)
    top = jnp.max(scores, axis=-1, keepdims=True)
    expo = jnp.where(causal, jnp.exp(scores - top), 0.0)
    probs = expo / jnp.sum(expo, axis=-1, keepdims=True)
    dprobs = lax.dot_general(grads, values, NT, preferred_element_type=F32)
    delta = jnp.sum(probs * dprobs, axis=-1, keepdims=True)
    dscore = (probs * (dprobs - delta) * scale).astype(BF)
    out_ref[0] = jnp.dot(dscore, keys, preferred_element_type=F32).astype(BF)
    out_ref[1] = lax.dot_general(dscore, query, TN, preferred_element_type=F32).astype(BF)
    out_ref[2] = lax.dot_general(probs.astype(BF), grads, TN, preferred_element_type=F32).astype(BF)


def attend(slopes, mine, theirs, ctx_grad, first, size):
    parts, length, width = mine.shape
    three = pl.BlockSpec((3, length, size), lambda head: (0, 0, head))
    return pl.pallas_call(
        functools.partial(attend_body, first, size ** (-0.5)),
        out_shape=jax.ShapeDtypeStruct((parts, length, width), BF),
        grid=(width // size,),
        in_specs=[SMEM, three, three, pl.BlockSpec((length, size), lambda head: (0, first + head))],
        out_specs=three,
        compiler_params=pltpu.CompilerParams(vmem_limit_bytes=LIMIT),
        cost_estimate=cost(10 * length * length * width, 14 * length * width),
        name="attend",
    )(slopes, mine, theirs, ctx_grad)


def back_body(chunks, sets, seeded, where_ref, *refs):
    pieces, refs = refs[: len(chunks)], refs[len(chunks) :]
    weights, refs = refs[:2], refs[2:]
    count = 2 * len(sets)
    seeds, outs = (refs[:count], refs[count:]) if seeded else (None, refs)
    width = outs[0].shape[1]
    for place, slot in enumerate(sets):
        for half in range(2):
            at = pl.ds(pl.multiple_of(where_ref[2 + half] * width, 128), width)
            out_ref = outs[2 * place + half]

            for side, weight in enumerate(weights):

                @pl.when(where_ref[slot] == side)
                def _(weight=weight, at=at, out_ref=out_ref, number=2 * place + half):
                    total = None
                    for (start, stop), piece in zip(chunks, pieces):
                        for part in range(3):
                            term = lax.dot_general(
                                piece[part], weight[part, at, start:stop], NT, preferred_element_type=F32
                            )
                            total = term if total is None else total + term
                    if seeded:
                        total = total + seeds[number][...]
                    out_ref[...] = total.astype(out_ref.dtype)


def back(where, pieces, chunks, weights, sets, dtypes, seeds=()):
    length = pieces[0].shape[1]
    width = weights[0].shape[2]
    depth = sum(stop - start for start, stop in chunks)
    count = 2 * len(sets)
    return pl.pallas_call(
        functools.partial(back_body, chunks, sets, bool(seeds)),
        out_shape=tuple(jax.ShapeDtypeStruct((length, width), dtypes[i // 2]) for i in range(count)),
        in_specs=[SMEM] + [VMEM] * (len(pieces) + 2 + len(seeds)),
        out_specs=(VMEM,) * count,
        compiler_params=pltpu.CompilerParams(vmem_limit_bytes=LIMIT),
        cost_estimate=cost(6 * length * count * width * depth, 6 * length * depth + 4 * count * length * width),
        name="back",
    )(where, *pieces, *weights, *seeds)


def on_device(checkpoint, projection, ctx_grad, slopes):
    dp = lax.axis_index("dp")
    tensor = lax.axis_index("tensor")
    core = dp & 1
    column_low = (tensor >> 1) & 1
    own_half = tensor & 1
    root = is_root(dp, tensor)
    side = jnp.where(root, column_low, 1 - column_low) ^ core
    where = jnp.stack([side, 1 - side, own_half, 1 - own_half]).astype(jnp.int32)

    heads = slopes.shape[0]
    size = ctx_grad.shape[3] // heads
    early = heads // 2
    columns = (early * size, (heads - early) * size)
    chunks = ((0, columns[0]), (columns[0], heads * size))

    after = lax.optimization_barrier
    own = checkpoint[0, 0]
    mine = jnp.transpose(projection[0], (1, 0, 2))
    theirs = exchange("theirs", mine, 1, 0)
    across = exchange("across", own, 0, 6)
    same = exchange("same", own, 0, 1, True)
    passed1 = jnp.where(root, across, own)
    passed2 = exchange("passed2", passed1, 0, 2)
    near1 = exchange("near1", passed1, 2, 0)
    far1 = exchange("far1", passed1, 2, 1)
    passed2, across, same, own = after((passed2, across, same, own))
    own1 = jnp.where(root, own, across)

    near2 = exchange("near2", passed2, 2, 0)
    far2 = exchange("far2", passed2, 2, 1)
    weights, sums = hold(passed2, where, (near1, far1), mine, theirs, chunks, 0)
    sums[0], own1, same = after((sums[0], own1, same))
    own2 = exchange("own2", own1, 0, 2)
    same1 = jnp.where(root, same, exchange("same1", same, 0, 6))
    same1, own2 = after((same1, own2))
    same2 = exchange("same2", same1, 0, 2)

    other = []
    for i in range(2):
        sent = project(where, (near2, far2), weights, chunks[i], 1, BF, sums[i])
        other.append(exchange(f"other{i}", sent, 2, 0))
    kept = [project(where, (own1, same1), weights, chunk, 0, F32) for chunk in chunks]
    kept = [project(where, (own2, same2), weights, chunks[i], 1, F32, kept[i]) for i in range(2)]
    grads = ctx_grad[0, 0]
    dqkv = [attend(slopes, kept[0], other[0], grads, 0, size)]
    partial = back(where, dqkv, chunks[:1], weights, (1,), (F32,))
    other[1], ready, kept[1], partial = after((other[1], dqkv[0], kept[1], partial))
    dqkv_other = [exchange("dqkv0", ready, 2, 0)]
    dqkv.append(attend(slopes, kept[1], other[1], grads, early, size))
    dqkv_other.append(exchange("dqkv1", dqkv[1], 2, 0))

    (sent0, sent1) = back(where, dqkv[1:], chunks[1:], weights, (1,), (BF,), partial)
    swap1 = exchange("own_swap1", sent1, 0, 2)
    swap0 = exchange("own_swap0", sent0, 0, 2)
    dqkv, first_arrived = after((dqkv, dqkv_other[0]))
    total = back(where, dqkv, chunks, weights, (0,), (F32,))
    seeds = back(where, (first_arrived,), chunks[:1], weights, (1, 0), (F32, F32))
    total1 = total[1] + swap1.astype(F32)
    total0 = total[0] + swap0.astype(F32)
    dqkv_other[1], _ = after((dqkv_other[1], total))
    second = back(where, dqkv_other[1:], chunks[1:], weights, (1,), (BF,), seeds[:2])
    second, seeds, total1, total0 = after((second, seeds, total1, total0))
    across1 = exchange("own_across1", total1.astype(BF), 0, 6)
    across0 = exchange("own_across0", total0.astype(BF), 0, 6)
    total1 = (total1 + across1.astype(F32)).astype(BF)
    far = exchange("own_far", total1, 0, 1, True)
    result_root = total0 + across0.astype(F32) + far.astype(F32)
    second = [exchange("second_near", second[0], 2, 0), exchange("second_far", second[1], 2, 1)]
    first = back(where, dqkv_other[1:], chunks[1:], weights, (0,), (BF,), seeds[2:])
    first = [exchange("first_near", first[0], 2, 0), exchange("first_far", first[1], 2, 1)]
    second = second[0].astype(F32) + second[1].astype(F32)
    swapped = exchange("swap", second.astype(BF), 0, 2)
    total = first[0].astype(F32) + first[1].astype(F32) + swapped.astype(F32)
    result = jnp.where(root, result_root, total).astype(BF)
    return (shift("shift", result) + shift("shift_across", total.astype(BF), 6, True))[None, None]


def solution(mesh):
    placed = (
        P("pipe", "dp", None, "tensor"),
        P("pipe", "dp", None, "tensor"),
        P("pipe", "dp", None, "tensor"),
        P("tensor"),
    )
    return jax.shard_map(
        on_device,
        mesh=mesh,
        in_specs=placed,
        out_specs=P("pipe", "dp", None, "tensor"),
        check_vma=False,
    )
```

```python
import functools

import jax
import jax.numpy as jnp
from jax import lax
from jax.experimental import pallas as pl
from jax.experimental.pallas import tpu as pltpu
from jax.sharding import PartitionSpec as P

F32 = jnp.float32
BF = jnp.bfloat16
VMEM = pl.BlockSpec(memory_space=pltpu.VMEM)
SMEM = pl.BlockSpec(memory_space=pltpu.SMEM)
NT = (((1,), (1,)), ((), ()))
TN = (((0,), (0,)), ((), ()))
LIMIT = 20 * 1024 * 1024


def cost(flops, size):
    return pl.CostEstimate(flops=flops // 20, bytes_accessed=size // 20, transcendentals=0)


def is_root(dp, tensor):
    return (tensor >> 2) == (dp >> 1)


def exchange(name, value, dp_flip, tensor_flip, senders=None):
    pairs = []
    for dp in range(4):
        for tensor in range(8):
            if senders is None or is_root(dp, tensor) == senders:
                pairs.append((dp * 8 + tensor, (dp ^ dp_flip) * 8 + (tensor ^ tensor_flip)))
    with jax.named_scope(name):
        return lax.ppermute(value, ("dp", "tensor"), pairs)


def shift(name, value, tensor_flip=0, senders=None):
    pipe = lax.axis_size("pipe")
    pairs = []
    for stage in range(pipe):
        for dp in range(4):
            for tensor in range(8):
                if senders is None or is_root(dp, tensor) == senders:
                    target = (dp * pipe + (stage - 1) % pipe) * 8 + (tensor ^ tensor_flip)
                    pairs.append(((dp * pipe + stage) * 8 + tensor, target))
    with jax.named_scope(name):
        return lax.ppermute(value, ("dp", "pipe", "tensor"), pairs)


def hold_body(columns, slot, after_ref, where_ref, near_ref, far_ref, mine_ref, theirs_ref, *refs):
    del after_ref
    held, out_refs, (rows_ref, sems) = refs[:2], refs[2:-2], refs[-2:]
    copies = [
        [
            pltpu.make_async_copy(source.at[part], target.at[part], sems.at[side, part])
            for side, (source, target) in enumerate(zip((mine_ref, theirs_ref), held))
        ]
        for part in range(3)
    ]
    for pair in copies[:2]:
        for copy in pair:
            copy.start()
    width = near_ref.shape[1]
    for place, ref in enumerate((near_ref, far_ref)):
        half = where_ref[2 + place]
        rows_ref[:, pl.ds(pl.multiple_of(half * width, 128), width)] = ref[...]
    for part, pair in enumerate(copies):
        for copy in pair:
            copy.wait()
        for copy in copies[part + 2] if part + 2 < len(copies) else ():
            copy.start()
        for side, weight in enumerate(held):

            @pl.when(where_ref[slot] == side)
            def _(weight=weight, part=part):
                for some, out_ref in zip(columns, out_refs):
                    out_ref[part] = jnp.dot(
                        rows_ref[...], weight[part, :, slice(*some)], preferred_element_type=F32
                    )


def hold(after, where, blocks, mine, theirs, columns, slot):
    hbm = pl.BlockSpec(memory_space=pltpu.HBM)
    length, width = blocks[0].shape
    mine_held, theirs_held, *sums = pl.pallas_call(
        functools.partial(hold_body, columns, slot),
        out_shape=(pltpu.VMEM(mine.shape, mine.dtype),) * 2
        + tuple(jax.ShapeDtypeStruct((3, length, stop - start), F32) for start, stop in columns),
        in_specs=[pl.BlockSpec(memory_space=pl.ANY), SMEM, VMEM, VMEM, hbm, hbm],
        out_specs=(VMEM,) * (2 + len(columns)),
        scratch_shapes=[pltpu.VMEM((length, 2 * width), BF), pltpu.SemaphoreType.DMA((2, 3))],
        compiler_params=pltpu.CompilerParams(vmem_limit_bytes=LIMIT),
        cost_estimate=cost(12 * length * width * 3 * width, 8 * mine.size),
        name="hold",
    )(
        after,
        where,
        *blocks,
        pltpu.with_memory_space_constraint(mine, pltpu.HBM),
        pltpu.with_memory_space_constraint(theirs, pltpu.HBM),
    )
    weights = tuple(
        pltpu.with_memory_space_constraint(value, pltpu.VMEM) for value in (mine_held, theirs_held)
    )
    return weights, sums


def project_body(columns, slot, seeded, where_ref, near_ref, far_ref, mine_ref, theirs_ref, *refs):
    width = near_ref.shape[1]
    seed_ref, out_ref, rows_ref = (refs[0] if seeded else None), refs[-2], refs[-1]
    for place, ref in enumerate((near_ref, far_ref)):
        half = where_ref[2 + place]
        rows_ref[:, pl.ds(pl.multiple_of(half * width, 128), width)] = ref[...]
    for side, weight in enumerate((mine_ref, theirs_ref)):

        @pl.when(where_ref[slot] == side)
        def _(weight=weight):
            for part in range(3):
                total = jnp.dot(rows_ref[...], weight[part, :, slice(*columns)], preferred_element_type=F32)
                if seeded:
                    total = total + seed_ref[part]
                out_ref[part] = total.astype(out_ref.dtype)


def project(where, blocks, weights, columns, slot, dtype, seed=None):
    length, width = blocks[0].shape
    some = columns[1] - columns[0]
    seeds = () if seed is None else (seed,)
    return pl.pallas_call(
        functools.partial(project_body, columns, slot, bool(seeds)),
        out_shape=jax.ShapeDtypeStruct((3, length, some), dtype),
        in_specs=[SMEM] + [VMEM] * (4 + len(seeds)),
        out_specs=VMEM,
        scratch_shapes=[pltpu.VMEM((length, 2 * width), BF)],
        compiler_params=pltpu.CompilerParams(vmem_limit_bytes=LIMIT),
        cost_estimate=cost(12 * length * width * some, 12 * length * some),
        name="project",
    )(where, *blocks, *weights, *seeds)


def attend_body(first, scale, slopes_ref, mine_ref, theirs_ref, ctx_ref, out_ref):
    length = mine_ref.shape[1]
    slope = slopes_ref[first + pl.program_id(0)]
    query, keys, values = (
        (mine_ref[part] + theirs_ref[part].astype(F32)).astype(BF) for part in range(3)
    )
    grads = ctx_ref[...]
    rows = lax.broadcasted_iota(jnp.int32, (length, length), 0)
    cols = lax.broadcasted_iota(jnp.int32, (length, length), 1)
    dist = (rows - cols).astype(F32)
    causal = rows >= cols
    scores = lax.dot_general(query, keys, NT, preferred_element_type=F32) * scale - slope * dist
    scores = jnp.where(causal, scores, -1e30)
    top = jnp.max(scores, axis=-1, keepdims=True)
    expo = jnp.where(causal, jnp.exp(scores - top), 0.0)
    probs = expo / jnp.sum(expo, axis=-1, keepdims=True)
    dprobs = lax.dot_general(grads, values, NT, preferred_element_type=F32)
    delta = jnp.sum(probs * dprobs, axis=-1, keepdims=True)
    dscore = (probs * (dprobs - delta) * scale).astype(BF)
    out_ref[0] = jnp.dot(dscore, keys, preferred_element_type=F32).astype(BF)
    out_ref[1] = lax.dot_general(dscore, query, TN, preferred_element_type=F32).astype(BF)
    out_ref[2] = lax.dot_general(probs.astype(BF), grads, TN, preferred_element_type=F32).astype(BF)


def attend(slopes, mine, theirs, ctx_grad, first, size):
    parts, length, width = mine.shape
    three = pl.BlockSpec((3, length, size), lambda head: (0, 0, head))
    return pl.pallas_call(
        functools.partial(attend_body, first, size ** (-0.5)),
        out_shape=jax.ShapeDtypeStruct((parts, length, width), BF),
        grid=(width // size,),
        in_specs=[SMEM, three, three, pl.BlockSpec((length, size), lambda head: (0, first + head))],
        out_specs=three,
        compiler_params=pltpu.CompilerParams(vmem_limit_bytes=LIMIT),
        cost_estimate=cost(10 * length * length * width, 14 * length * width),
        name="attend",
    )(slopes, mine, theirs, ctx_grad)


def back_body(chunks, sets, seeded, where_ref, *refs):
    pieces, refs = refs[: len(chunks)], refs[len(chunks) :]
    weights, refs = refs[:2], refs[2:]
    count = 2 * len(sets)
    seeds, outs = (refs[:count], refs[count:]) if seeded else (None, refs)
    width = outs[0].shape[1]
    for place, slot in enumerate(sets):
        for half in range(2):
            at = pl.ds(pl.multiple_of(where_ref[2 + half] * width, 128), width)
            out_ref = outs[2 * place + half]

            for side, weight in enumerate(weights):

                @pl.when(where_ref[slot] == side)
                def _(weight=weight, at=at, out_ref=out_ref, number=2 * place + half):
                    total = None
                    for (start, stop), piece in zip(chunks, pieces):
                        for part in range(3):
                            term = lax.dot_general(
                                piece[part], weight[part, at, start:stop], NT, preferred_element_type=F32
                            )
                            total = term if total is None else total + term
                    if seeded:
                        total = total + seeds[number][...]
                    out_ref[...] = total.astype(out_ref.dtype)


def back(where, pieces, chunks, weights, sets, dtypes, seeds=()):
    length = pieces[0].shape[1]
    width = weights[0].shape[2]
    depth = sum(stop - start for start, stop in chunks)
    count = 2 * len(sets)
    return pl.pallas_call(
        functools.partial(back_body, chunks, sets, bool(seeds)),
        out_shape=tuple(jax.ShapeDtypeStruct((length, width), dtypes[i // 2]) for i in range(count)),
        in_specs=[SMEM] + [VMEM] * (len(pieces) + 2 + len(seeds)),
        out_specs=(VMEM,) * count,
        compiler_params=pltpu.CompilerParams(vmem_limit_bytes=LIMIT),
        cost_estimate=cost(6 * length * count * width * depth, 6 * length * depth + 4 * count * length * width),
        name="back",
    )(where, *pieces, *weights, *seeds)


def on_device(checkpoint, projection, ctx_grad, slopes):
    dp = lax.axis_index("dp")
    tensor = lax.axis_index("tensor")
    core = dp & 1
    column_low = (tensor >> 1) & 1
    own_half = tensor & 1
    root = is_root(dp, tensor)
    side = jnp.where(root, column_low, 1 - column_low) ^ core
    where = jnp.stack([side, 1 - side, own_half, 1 - own_half]).astype(jnp.int32)

    heads = slopes.shape[0]
    size = ctx_grad.shape[3] // heads
    early = heads // 2
    columns = (early * size, (heads - early) * size)
    chunks = ((0, columns[0]), (columns[0], heads * size))

    after = lax.optimization_barrier
    own = checkpoint[0, 0]
    mine = jnp.transpose(projection[0], (1, 0, 2))
    theirs = exchange("theirs", mine, 1, 0)
    across = exchange("across", own, 0, 6)
    same = exchange("same", own, 0, 1, True)
    passed1 = jnp.where(root, across, own)
    passed2 = exchange("passed2", passed1, 0, 2)
    near1 = exchange("near1", passed1, 2, 0)
    far1 = exchange("far1", passed1, 2, 1)
    passed2, across, same, own = after((passed2, across, same, own))
    own1 = jnp.where(root, own, across)

    near2 = exchange("near2", passed2, 2, 0)
    far2 = exchange("far2", passed2, 2, 1)
    weights, sums = hold(passed2, where, (near1, far1), mine, theirs, chunks, 0)
    sums[0], own1, same = after((sums[0], own1, same))
    own2 = exchange("own2", own1, 0, 2)
    same1 = jnp.where(root, same, exchange("same1", same, 0, 6))
    same1, own2 = after((same1, own2))
    same2 = exchange("same2", same1, 0, 2)

    other = []
    for i in range(2):
        sent = project(where, (near2, far2), weights, chunks[i], 1, BF, sums[i])
        other.append(exchange(f"other{i}", sent, 2, 0))
    kept = [project(where, (own1, same1), weights, chunk, 0, F32) for chunk in chunks]
    kept = [project(where, (own2, same2), weights, chunks[i], 1, F32, kept[i]) for i in range(2)]
    grads = ctx_grad[0, 0]
    dqkv = [attend(slopes, kept[0], other[0], grads, 0, size)]
    partial = back(where, dqkv, chunks[:1], weights, (1,), (F32,))
    other[1], ready, kept[1], partial = after((other[1], dqkv[0], kept[1], partial))
    dqkv_other = [exchange("dqkv0", ready, 2, 0)]
    dqkv.append(attend(slopes, kept[1], other[1], grads, early, size))
    dqkv_other.append(exchange("dqkv1", dqkv[1], 2, 0))

    (sent0, sent1) = back(where, dqkv[1:], chunks[1:], weights, (1,), (BF,), partial)
    swap1 = exchange("own_swap1", sent1, 0, 2)
    swap0 = exchange("own_swap0", sent0, 0, 2)
    dqkv, first_arrived = after((dqkv, dqkv_other[0]))
    total = back(where, dqkv, chunks, weights, (0,), (F32,))
    seeds = back(where, (first_arrived,), chunks[:1], weights, (1, 0), (F32, F32))
    total1 = total[1] + swap1.astype(F32)
    total0 = total[0] + swap0.astype(F32)
    dqkv_other[1], _ = after((dqkv_other[1], total))
    second = back(where, dqkv_other[1:], chunks[1:], weights, (1,), (BF,), seeds[:2])
    second, seeds, total0 = after((second, seeds, total0))
    across1 = exchange("own_across1", total1.astype(BF), 0, 6)
    across0 = exchange("own_across0", total0.astype(BF), 0, 6)
    total1 = (total1 + across1.astype(F32)).astype(BF)
    far = exchange("own_far", total1, 0, 1, True)
    result_root = total0 + across0.astype(F32) + far.astype(F32)
    second = [exchange("second_near", second[0], 2, 0), exchange("second_far", second[1], 2, 1)]
    first = back(where, dqkv_other[1:], chunks[1:], weights, (0,), (BF,), seeds[2:])
    first = [exchange("first_near", first[0], 2, 0), exchange("first_far", first[1], 2, 1)]
    second = second[0].astype(F32) + second[1].astype(F32)
    swapped = exchange("swap", second.astype(BF), 0, 2)
    total = first[0].astype(F32) + first[1].astype(F32) + swapped.astype(F32)
    result = jnp.where(root, result_root, total).astype(BF)
    return (shift("shift", result) + shift("shift_across", total.astype(BF), 6, True))[None, None]


def solution(mesh):
    placed = (
        P("pipe", "dp", None, "tensor"),
        P("pipe", "dp", None, "tensor"),
        P("pipe", "dp", None, "tensor"),
        P("tensor"),
    )
    return jax.shard_map(
        on_device,
        mesh=mesh,
        in_specs=placed,
        out_specs=P("pipe", "dp", None, "tensor"),
        check_vma=False,
    )
```

```python
import functools

import jax
import jax.numpy as jnp
from jax import lax
from jax.experimental import pallas as pl
from jax.experimental.pallas import tpu as pltpu
from jax.sharding import PartitionSpec as P

F32 = jnp.float32
BF = jnp.bfloat16
VMEM = pl.BlockSpec(memory_space=pltpu.VMEM)
SMEM = pl.BlockSpec(memory_space=pltpu.SMEM)
NT = (((1,), (1,)), ((), ()))
TN = (((0,), (0,)), ((), ()))
LIMIT = 20 * 1024 * 1024


def cost(flops, size):
    return pl.CostEstimate(flops=flops // 20, bytes_accessed=size // 20, transcendentals=0)


def is_root(dp, tensor):
    return (tensor >> 2) == (dp >> 1)


def exchange(name, value, dp_flip, tensor_flip, senders=None):
    pairs = []
    for dp in range(4):
        for tensor in range(8):
            if senders is None or is_root(dp, tensor) == senders:
                pairs.append((dp * 8 + tensor, (dp ^ dp_flip) * 8 + (tensor ^ tensor_flip)))
    with jax.named_scope(name):
        return lax.ppermute(value, ("dp", "tensor"), pairs)


def shift(name, value, tensor_flip=0, senders=None):
    pipe = lax.axis_size("pipe")
    pairs = []
    for stage in range(pipe):
        for dp in range(4):
            for tensor in range(8):
                if senders is None or is_root(dp, tensor) == senders:
                    target = (dp * pipe + (stage - 1) % pipe) * 8 + (tensor ^ tensor_flip)
                    pairs.append(((dp * pipe + stage) * 8 + tensor, target))
    with jax.named_scope(name):
        return lax.ppermute(value, ("dp", "pipe", "tensor"), pairs)


def hold_body(columns, slot, after_ref, where_ref, near_ref, far_ref, mine_ref, theirs_ref, *refs):
    del after_ref
    held, out_refs, (rows_ref, sems) = refs[:2], refs[2:-2], refs[-2:]
    copies = [
        [
            pltpu.make_async_copy(source.at[part], target.at[part], sems.at[side, part])
            for side, (source, target) in enumerate(zip((mine_ref, theirs_ref), held))
        ]
        for part in range(3)
    ]
    for pair in copies[:2]:
        for copy in pair:
            copy.start()
    width = near_ref.shape[1]
    for place, ref in enumerate((near_ref, far_ref)):
        half = where_ref[2 + place]
        rows_ref[:, pl.ds(pl.multiple_of(half * width, 128), width)] = ref[...]
    for part, pair in enumerate(copies):
        for copy in pair:
            copy.wait()
        for copy in copies[part + 2] if part + 2 < len(copies) else ():
            copy.start()
        for side, weight in enumerate(held):

            @pl.when(where_ref[slot] == side)
            def _(weight=weight, part=part):
                for some, out_ref in zip(columns, out_refs):
                    out_ref[part] = jnp.dot(
                        rows_ref[...], weight[part, :, slice(*some)], preferred_element_type=F32
                    )


def hold(after, where, blocks, mine, theirs, columns, slot):
    hbm = pl.BlockSpec(memory_space=pltpu.HBM)
    length, width = blocks[0].shape
    mine_held, theirs_held, *sums = pl.pallas_call(
        functools.partial(hold_body, columns, slot),
        out_shape=(pltpu.VMEM(mine.shape, mine.dtype),) * 2
        + tuple(jax.ShapeDtypeStruct((3, length, stop - start), F32) for start, stop in columns),
        in_specs=[pl.BlockSpec(memory_space=pl.ANY), SMEM, VMEM, VMEM, hbm, hbm],
        out_specs=(VMEM,) * (2 + len(columns)),
        scratch_shapes=[pltpu.VMEM((length, 2 * width), BF), pltpu.SemaphoreType.DMA((2, 3))],
        compiler_params=pltpu.CompilerParams(vmem_limit_bytes=LIMIT),
        cost_estimate=cost(12 * length * width * 3 * width, 8 * mine.size),
        name="hold",
    )(
        after,
        where,
        *blocks,
        pltpu.with_memory_space_constraint(mine, pltpu.HBM),
        pltpu.with_memory_space_constraint(theirs, pltpu.HBM),
    )
    weights = tuple(
        pltpu.with_memory_space_constraint(value, pltpu.VMEM) for value in (mine_held, theirs_held)
    )
    return weights, sums


def project_body(columns, slot, seeded, where_ref, near_ref, far_ref, mine_ref, theirs_ref, *refs):
    width = near_ref.shape[1]
    seed_ref, out_ref, rows_ref = (refs[0] if seeded else None), refs[-2], refs[-1]
    for place, ref in enumerate((near_ref, far_ref)):
        half = where_ref[2 + place]
        rows_ref[:, pl.ds(pl.multiple_of(half * width, 128), width)] = ref[...]
    for side, weight in enumerate((mine_ref, theirs_ref)):

        @pl.when(where_ref[slot] == side)
        def _(weight=weight):
            for part in range(3):
                total = jnp.dot(rows_ref[...], weight[part, :, slice(*columns)], preferred_element_type=F32)
                if seeded:
                    total = total + seed_ref[part]
                out_ref[part] = total.astype(out_ref.dtype)


def project(where, blocks, weights, columns, slot, dtype, seed=None):
    length, width = blocks[0].shape
    some = columns[1] - columns[0]
    seeds = () if seed is None else (seed,)
    return pl.pallas_call(
        functools.partial(project_body, columns, slot, bool(seeds)),
        out_shape=jax.ShapeDtypeStruct((3, length, some), dtype),
        in_specs=[SMEM] + [VMEM] * (4 + len(seeds)),
        out_specs=VMEM,
        scratch_shapes=[pltpu.VMEM((length, 2 * width), BF)],
        compiler_params=pltpu.CompilerParams(vmem_limit_bytes=LIMIT),
        cost_estimate=cost(12 * length * width * some, 12 * length * some),
        name="project",
    )(where, *blocks, *weights, *seeds)


def attend_body(first, scale, slopes_ref, mine_ref, theirs_ref, ctx_ref, out_ref):
    length = mine_ref.shape[1]
    slope = slopes_ref[first + pl.program_id(0)]
    query, keys, values = (
        (mine_ref[part] + theirs_ref[part].astype(F32)).astype(BF) for part in range(3)
    )
    grads = ctx_ref[...]
    rows = lax.broadcasted_iota(jnp.int32, (length, length), 0)
    cols = lax.broadcasted_iota(jnp.int32, (length, length), 1)
    dist = (rows - cols).astype(F32)
    causal = rows >= cols
    scores = lax.dot_general(query, keys, NT, preferred_element_type=F32) * scale - slope * dist
    scores = jnp.where(causal, scores, -1e30)
    top = jnp.max(scores, axis=-1, keepdims=True)
    expo = jnp.where(causal, jnp.exp(scores - top), 0.0)
    probs = expo / jnp.sum(expo, axis=-1, keepdims=True)
    dprobs = lax.dot_general(grads, values, NT, preferred_element_type=F32)
    delta = jnp.sum(probs * dprobs, axis=-1, keepdims=True)
    dscore = (probs * (dprobs - delta) * scale).astype(BF)
    out_ref[0] = jnp.dot(dscore, keys, preferred_element_type=F32).astype(BF)
    out_ref[1] = lax.dot_general(dscore, query, TN, preferred_element_type=F32).astype(BF)
    out_ref[2] = lax.dot_general(probs.astype(BF), grads, TN, preferred_element_type=F32).astype(BF)


def attend(slopes, mine, theirs, ctx_grad, first, size):
    parts, length, width = mine.shape
    three = pl.BlockSpec((3, length, size), lambda head: (0, 0, head))
    return pl.pallas_call(
        functools.partial(attend_body, first, size ** (-0.5)),
        out_shape=jax.ShapeDtypeStruct((parts, length, width), BF),
        grid=(width // size,),
        in_specs=[SMEM, three, three, pl.BlockSpec((length, size), lambda head: (0, first + head))],
        out_specs=three,
        compiler_params=pltpu.CompilerParams(vmem_limit_bytes=LIMIT),
        cost_estimate=cost(10 * length * length * width, 14 * length * width),
        name="attend",
    )(slopes, mine, theirs, ctx_grad)


def back_body(chunks, sets, seeded, where_ref, *refs):
    pieces, refs = refs[: len(chunks)], refs[len(chunks) :]
    weights, refs = refs[:2], refs[2:]
    count = 2 * len(sets)
    seeds, outs = (refs[:count], refs[count:]) if seeded else (None, refs)
    width = outs[0].shape[1]
    for place, slot in enumerate(sets):
        for half in range(2):
            at = pl.ds(pl.multiple_of(where_ref[2 + half] * width, 128), width)
            out_ref = outs[2 * place + half]

            for side, weight in enumerate(weights):

                @pl.when(where_ref[slot] == side)
                def _(weight=weight, at=at, out_ref=out_ref, number=2 * place + half):
                    total = None
                    for (start, stop), piece in zip(chunks, pieces):
                        for part in range(3):
                            term = lax.dot_general(
                                piece[part], weight[part, at, start:stop], NT, preferred_element_type=F32
                            )
                            total = term if total is None else total + term
                    if seeded:
                        total = total + seeds[number][...]
                    out_ref[...] = total.astype(out_ref.dtype)


def back(where, pieces, chunks, weights, sets, dtypes, seeds=()):
    length = pieces[0].shape[1]
    width = weights[0].shape[2]
    depth = sum(stop - start for start, stop in chunks)
    count = 2 * len(sets)
    return pl.pallas_call(
        functools.partial(back_body, chunks, sets, bool(seeds)),
        out_shape=tuple(jax.ShapeDtypeStruct((length, width), dtypes[i // 2]) for i in range(count)),
        in_specs=[SMEM] + [VMEM] * (len(pieces) + 2 + len(seeds)),
        out_specs=(VMEM,) * count,
        compiler_params=pltpu.CompilerParams(vmem_limit_bytes=LIMIT),
        cost_estimate=cost(6 * length * count * width * depth, 6 * length * depth + 4 * count * length * width),
        name="back",
    )(where, *pieces, *weights, *seeds)


def on_device(checkpoint, projection, ctx_grad, slopes):
    dp = lax.axis_index("dp")
    tensor = lax.axis_index("tensor")
    core = dp & 1
    column_low = (tensor >> 1) & 1
    own_half = tensor & 1
    root = is_root(dp, tensor)
    side = jnp.where(root, column_low, 1 - column_low) ^ core
    where = jnp.stack([side, 1 - side, own_half, 1 - own_half]).astype(jnp.int32)

    heads = slopes.shape[0]
    size = ctx_grad.shape[3] // heads
    early = heads // 2
    columns = (early * size, (heads - early) * size)
    chunks = ((0, columns[0]), (columns[0], heads * size))

    after = lax.optimization_barrier
    own = checkpoint[0, 0]
    mine = jnp.transpose(projection[0], (1, 0, 2))
    theirs = exchange("theirs", mine, 1, 0)
    across = exchange("across", own, 0, 6)
    same = exchange("same", own, 0, 1, True)
    passed1 = jnp.where(root, across, own)
    passed2 = exchange("passed2", passed1, 0, 2)
    near1 = exchange("near1", passed1, 2, 0)
    far1 = exchange("far1", passed1, 2, 1)
    passed2, across, same, own = after((passed2, across, same, own))
    own1 = jnp.where(root, own, across)

    near2 = exchange("near2", passed2, 2, 0)
    far2 = exchange("far2", passed2, 2, 1)
    weights, sums = hold(passed2, where, (near1, far1), mine, theirs, chunks, 0)
    sums[0], own1, same = after((sums[0], own1, same))
    own2 = exchange("own2", own1, 0, 2)
    same1 = jnp.where(root, same, exchange("same1", same, 0, 6))
    same1, own2 = after((same1, own2))
    same2 = exchange("same2", same1, 0, 2)

    other = []
    for i in range(2):
        sent = project(where, (near2, far2), weights, chunks[i], 1, BF, sums[i])
        other.append(exchange(f"other{i}", sent, 2, 0))
    kept = [project(where, (own1, same1), weights, chunk, 0, F32) for chunk in chunks]
    kept = [project(where, (own2, same2), weights, chunks[i], 1, F32, kept[i]) for i in range(2)]
    grads = ctx_grad[0, 0]
    dqkv = [attend(slopes, kept[0], other[0], grads, 0, size)]
    partial = back(where, dqkv, chunks[:1], weights, (1,), (F32,))
    other[1], ready, kept[1], partial = after((other[1], dqkv[0], kept[1], partial))
    dqkv_other = [exchange("dqkv0", ready, 2, 0)]
    dqkv.append(attend(slopes, kept[1], other[1], grads, early, size))
    dqkv_other.append(exchange("dqkv1", dqkv[1], 2, 0))

    (sent0, sent1) = back(where, dqkv[1:], chunks[1:], weights, (1,), (BF,), partial)
    swap1 = exchange("own_swap1", sent1, 0, 2)
    swap0 = exchange("own_swap0", sent0, 0, 2)
    dqkv, first_arrived = after((dqkv, dqkv_other[0]))
    total = back(where, dqkv, chunks, weights, (0,), (F32,))
    seeds = back(where, (first_arrived,), chunks[:1], weights, (1, 0), (F32, F32))
    total1 = total[1] + swap1.astype(F32)
    total0 = total[0] + swap0.astype(F32)
    dqkv_other[1], _ = after((dqkv_other[1], total))
    second = back(where, dqkv_other[1:], chunks[1:], weights, (1,), (BF,), seeds[:2])
    second, seeds, total0 = after((second, seeds, total0))
    across1 = exchange("own_across1", total1.astype(BF), 0, 6)
    across0 = exchange("own_across0", total0.astype(BF), 0, 6)
    total1 = (total1 + across1.astype(F32)).astype(BF)
    far = exchange("own_far", total1, 0, 1)
    result_root = total0 + across0.astype(F32) + far.astype(F32)
    second = [exchange("second_near", second[0], 2, 0), exchange("second_far", second[1], 2, 1)]
    first = back(where, dqkv_other[1:], chunks[1:], weights, (0,), (BF,), seeds[2:])
    first = [exchange("first_near", first[0], 2, 0), exchange("first_far", first[1], 2, 1)]
    second = second[0].astype(F32) + second[1].astype(F32)
    swapped = exchange("swap", second.astype(BF), 0, 2)
    total = first[0].astype(F32) + first[1].astype(F32) + swapped.astype(F32)
    result = jnp.where(root, result_root, total).astype(BF)
    return (shift("shift", result) + shift("shift_across", total.astype(BF), 6, True))[None, None]


def solution(mesh):
    placed = (
        P("pipe", "dp", None, "tensor"),
        P("pipe", "dp", None, "tensor"),
        P("pipe", "dp", None, "tensor"),
        P("tensor"),
    )
    return jax.shard_map(
        on_device,
        mesh=mesh,
        in_specs=placed,
        out_specs=P("pipe", "dp", None, "tensor"),
        check_vma=False,
    )
```
